512 devices in a mesh: slab: 128 (over y, z, core), grp: 4 (over x).
Axes of the slice: x: 4, y: 8, z: 8, core: 2. Of those that a mesh axis runs over, the one named last changes fastest.
Arguments:
- a_blocks: bfloat16 [28672, 8, 64, 64], P(('slab', 'grp')), may hold values from -0.25 to 0.25
- neighbors: int32 [28672, 8], P(('slab', 'grp')), may hold values from 0 to 167, as said below
- prolong: bfloat16 [28672, 64, 64], P(('slab', 'grp')), may hold values from -2 to 2
- agg_ids: int32 [28672], P(('slab', 'grp')), may hold values from 0 to 7167, as said below
- coarse_prolong: bfloat16 [7168, 64, 64], P(('slab', 'grp')), may hold values from -0.75 to 0.75
- pairing: int32 [512, 7], P(('slab', 'grp')), may hold values from 0 to 13, as said below
Outputs:
- coarse_one: float32 [7168, 64, 64], P(('slab', 'grp'))
- coarse_two: float32 [3584, 64, 64], P(('slab', 'grp'))
The draws below stay inside these ranges and needn't reach their ends.
Inputs may be any that keep to these rules, and one draw needn't show every extreme that they name: neighbors[r, 0] is the row itself, 56 + r % 56. The aggregate of a row is owned by a device of the same grp index: agg_ids[r] // 14 % 4 equals the grp index of the row's shard; its owner slab index agg_ids[r] // (14 * 4) lies in the five slabs from min(max(s - 2, 0), 128 - 5) on, where s is the slab index of the row's shard; the rows of one shard name at most 12 rows for one owner slab index, and that number is reached on every shard. `pairing`: rows s * 4 + 2h and s * 4 + 2h + 1 together hold each of 0 to 13 once.
All inputs are finite; a program needn't handle non-finite values.
Results may differ from the reference program's by a relative error of at most 0.0029.
Values may be sent and summed in bfloat16 or wider, within the bound.
A program may use at most 64 MiB of HBM per device.

```python
import jax
import jax.numpy as jnp
from jax import lax

BS = 64
NB = 8
ROWS_DEV = 56
AGG_DEV = 14
FINE = 28672
AGG1 = 7168
AGG2 = 3584
N_SLAB = 128
N_GRP = 4


def draw_neighbors(key, part):
    key = jax.random.fold_in(key, 1)
    total = ROWS_DEV * N_SLAB * N_GRP
    others = jax.random.randint(key, (total, NB - 1), 0, 3 * ROWS_DEV)
    itself = ROWS_DEV + jnp.arange(total) % ROWS_DEV
    return jnp.concatenate([itself[:, None], others], 1).astype(jnp.int32)


def draw_agg_ids(key, part):
    key = jax.random.fold_in(key, 2)
    shards = N_SLAB * N_GRP
    repeats = (ROWS_DEV + 4) // 5

    def one_shard(subkey, shard):
        first, second, third = jax.random.split(subkey, 3)
        slab_at = shard // N_GRP
        window = jnp.clip(slab_at - 2, 0, N_SLAB - 5)
        offsets = jnp.tile(jax.random.permutation(first, 5), repeats)[:ROWS_DEV]
        offsets = jax.random.permutation(second, offsets)
        owners = window + offsets
        inside = jax.random.randint(third, (ROWS_DEV,), 0, AGG_DEV)
        return (owners * N_GRP + shard % N_GRP) * AGG_DEV + inside
    keys = jax.random.split(key, shards)
    return jax.vmap(one_shard)(keys, jnp.arange(shards)).reshape(-1).astype(jnp.int32)


def draw_pairing(key, part):
    key = jax.random.fold_in(key, 3)
    pairs = N_SLAB * N_GRP // 2
    keys = jax.random.split(key, pairs)
    perms = jax.vmap(lambda subkey: jax.random.permutation(subkey, AGG_DEV))(keys)
    return perms.reshape(pairs * 2, AGG_DEV // 2).astype(jnp.int32)


def block_levels(own_key, shape, cuts, least, top_value):
    def one(axis_at, shards_of):
        draws = jax.random.uniform(jax.random.fold_in(jax.random.fold_in(own_key, 6), axis_at), (shards_of,), jnp.float32, least / len(cuts), top_value / len(cuts))
        return jnp.repeat(jnp.exp(draws), shape[axis_at] // shards_of).reshape((-1,) + (1,) * (len(shape) - axis_at - 1))

    level = one(*cuts[0])
    for cut in cuts[1:]:
        level = level * one(*cut)
    return level


def gaussian(own_key, dims, deviation, reach, cuts=(), kind=jnp.bfloat16):
    array = deviation * jax.random.normal(own_key, dims, jnp.float32)
    if cuts:
        array = array * block_levels(own_key, dims, cuts, -0.22, 0.18)
    return jnp.clip(array, -reach, reach).astype(kind)


def setup_inputs(seed: int = 0) -> dict:
    key_of = jax.random.split(jax.random.key(seed), 7)
    return {
        "a_blocks": gaussian(key_of[0], (FINE, NB, BS, BS), (NB * BS) ** -0.5, 0.25, ((0, 512),)),
        "neighbors": draw_neighbors(jax.random.fold_in(key_of[6], 71), 0),
        "prolong": gaussian(key_of[2], (FINE, BS, BS), 0.35, 2.0, ((0, 512),)),
        "agg_ids": draw_agg_ids(jax.random.fold_in(key_of[6], 71), 0),
        "coarse_prolong": gaussian(key_of[4], (AGG1, BS, BS), BS ** -0.5, 0.75, ((0, 512),)),
        "pairing": draw_pairing(jax.random.fold_in(key_of[6], 71), 0),
    }


def galerkin(blocks, maps):
    inner = jnp.einsum('kbc,kcd->kbd', blocks, maps, precision=lax.Precision.HIGHEST)
    return jnp.einsum('kba,kbd->kad', maps, inner, precision=lax.Precision.HIGHEST)


def reference(a_blocks, neighbors, prolong, agg_ids, coarse_prolong, pairing):
    shards = N_SLAB * N_GRP
    a_dev = a_blocks.reshape(shards, ROWS_DEV, NB, BS, BS)
    nb_dev = neighbors.reshape(shards, ROWS_DEV, NB)
    p_dev = prolong.reshape(shards, ROWS_DEV, BS, BS)
    agg_dev = agg_ids.reshape(shards, ROWS_DEV)

    def one_shard(carry, inputs):
        shard, a_rows, nb_rows, p_rows, agg_rows = inputs
        slab_at = shard // N_GRP
        grp_at = shard % N_GRP
        source = slab_at + nb_rows // ROWS_DEV - 1
        valid = ((source >= 0) & (source < N_SLAB)).astype(jnp.float32)
        clipped = jnp.clip(source, 0, N_SLAB - 1)
        global_rows = ((clipped * N_GRP + grp_at) * ROWS_DEV + nb_rows % ROWS_DEV).astype(jnp.int32)
        picked = prolong[global_rows].astype(jnp.float32) * valid[:, :, None, None]
        partial_w = jnp.einsum('rnab,rnbc->rac', a_rows.astype(jnp.float32), picked).astype(jnp.bfloat16)
        parts = jnp.einsum('rba,rbc->rac', p_rows.astype(jnp.float32), partial_w.astype(jnp.float32))
        return carry.at[agg_rows].add(parts), None

    start = jnp.zeros((AGG1, BS, BS), jnp.float32)
    shard_ids = jnp.arange(shards, dtype=jnp.int32)
    coarse_one = lax.scan(one_shard, start, (shard_ids, a_dev, nb_dev, p_dev, agg_dev))[0]
    terms = galerkin(coarse_one, coarse_prolong.astype(jnp.float32))
    grouped = terms.reshape(N_SLAB, N_GRP // 2, 2, AGG_DEV, BS, BS)
    paired = pairing.reshape(N_SLAB, N_GRP // 2, AGG_DEV)
    odd_terms = jnp.take_along_axis(grouped[:, :, 1], paired[:, :, :, None, None], axis=2)
    coarse_two = (grouped[:, :, 0] + odd_terms).reshape(AGG2, BS, BS)
    return coarse_one, coarse_two
```

```python
import functools

import jax
import jax.numpy as jnp
from jax import lax
from jax.experimental import pallas as pl
from jax.experimental.pallas import tpu as pltpu
from jax.sharding import PartitionSpec as P

MESH = pl.DeviceIdType.MESH
WINDOW = 5
REACH = WINDOW - 1
CHUNKS = 4
F32 = jnp.float32
BF16 = jnp.bfloat16


def fold(block):
    half = block.shape[0] // 2
    return jnp.concatenate([block[:half], block[half:]], axis=1)


def unfold(block):
    width = block.shape[1] // 2
    return jnp.concatenate([block[:, :width], block[:, width:]], axis=0)


def galerkin(block, map_t, map_):
    high = block.astype(BF16)
    low = (block - high.astype(F32)).astype(BF16)
    inner = jnp.dot(map_t, high, preferred_element_type=F32) + jnp.dot(
        map_t, low, preferred_element_type=F32
    )
    high = inner.astype(BF16)
    low = (inner - high.astype(F32)).astype(BF16)
    return jnp.dot(high, map_, preferred_element_type=F32) + jnp.dot(
        low, map_, preferred_element_type=F32
    )


def kernel(
    sizes,
    nbr, agg, pair, a_hbm, p_hbm, m_hbm,
    one_hbm, two_hbm,
    a_buf, a_cat, ext, p_fold, halo, p_t, m_buf, m_t, run, send, recv, acc, one_buf, two_buf, tx, rx, tab_v, tab,
    a_sem, in_sem, tab_sem, out_sem, halo_send, halo_recv, part_send, part_recv, pair_send, pair_recv,
):
    n_slab, n_grp, rows, slots, width, aggs = sizes
    half = aggs // 2
    capacity = (rows + WINDOW - 1) // WINDOW
    slab = lax.axis_index("slab")
    grp = lax.axis_index("grp")

    def window(s):
        return jnp.clip(s - WINDOW // 2, 0, n_slab - WINDOW)

    first = window(slab)
    chip_mate = slab + 1 - 2 * (slab % 2)
    grp_mate = grp + 1 - 2 * (grp % 2)
    parity = grp % 2

    p_copy = pltpu.make_async_copy(p_hbm, ext.at[pl.ds(rows, rows)], in_sem.at[0])
    p_copy.start()
    m_copy = pltpu.make_async_copy(m_hbm, m_buf, in_sem.at[1])
    a_chunks = a_sem.shape[0]
    a_rows = rows // a_chunks
    a_copies = [
        pltpu.make_async_copy(a_hbm.at[pl.ds(i * a_rows, a_rows)], a_buf.at[pl.ds(i * a_rows, a_rows)], a_sem.at[i])
        for i in range(a_chunks)
    ]
    for copy in a_copies:
        copy.start()
    m_copy.start()

    barrier = pltpu.get_barrier_semaphore()

    def sends_here(offset):
        source = slab + offset
        low = window(source)
        return (source >= 0) & (source < n_slab) & (low <= slab) & (slab < low + WINDOW)

    for offset in range(-REACH, REACH + 1):
        if offset != 0:
            @pl.when(sends_here(offset))
            def _():
                pl.semaphore_signal(barrier, inc=1, device_id=(slab + offset, grp), device_id_type=MESH)
    pl.semaphore_signal(barrier, inc=1, device_id=(slab, grp_mate), device_id_type=MESH)

    p_copy.wait()
    per = rows // CHUNKS

    def halo_copy(side, chunk):
        span = pl.ds(chunk * per, per)
        target = slab + 1 - 2 * side
        return pltpu.make_async_remote_copy(
            src_ref=p_fold.at[span],
            dst_ref=halo.at[side, span],
            send_sem=halo_send.at[side, chunk],
            recv_sem=halo_recv.at[side, chunk],
            device_id=(target, grp),
            device_id_type=MESH,
        )

    has_next = slab < n_slab - 1
    has_previous = slab > 0
    for chunk in range(CHUNKS):
        def fold_row(r, _, chunk=chunk):
            p_fold[chunk * per + r] = fold(ext[rows + chunk * per + r])
            return 0

        lax.fori_loop(0, per, fold_row, 0, unroll=2)
        if chunk == 0:
            pl.semaphore_wait(barrier, WINDOW)

        @pl.when(has_next)
        def _():
            halo_copy(0, chunk).start()

        @pl.when(has_previous)
        def _():
            halo_copy(1, chunk).start()

    tag = []
    for j in range(WINDOW):
        owner = first + j
        kind = jnp.where(owner == slab, 2, jnp.where(owner == chip_mate, 1, 0))
        tag.append(kind * WINDOW + j)
    place = [sum((tag[i] < tag[j]).astype(jnp.int32) for i in range(WINDOW)) for j in range(WINDOW)]
    bucket_of = [
        sum(jnp.where(place[j] == q, j, 0) for j in range(WINDOW)) for q in range(WINDOW)
    ]
    tall = 64
    sub = lax.broadcasted_iota(jnp.int32, (tall, 128), 0)
    lane = lax.broadcasted_iota(jnp.int32, (tall, 128), 1)
    lane_row = lax.broadcasted_iota(jnp.int32, (1, 128), 1)
    tab_v[...] = jnp.zeros_like(tab_v)
    tab_v[0:1, 0:rows] = agg[...]
    ids = tab_v[0:1, :]
    owner_row = lax.div(ids, jnp.int32(n_grp * aggs))
    inside = lax.rem(ids, jnp.int32(aggs))
    bucket = owner_row - first
    at = jnp.zeros_like(bucket)
    for j in range(WINDOW):
        at = at + jnp.where(bucket == j, place[j], 0)
    far = 1000
    key_row = jnp.where(lane_row < rows, at * aggs + inside, far).astype(F32)
    keys = jnp.broadcast_to(key_row, (tall, 128))
    key_col = jnp.sum(jnp.where(sub == lane, keys, 0.0), axis=1, keepdims=True)
    less = (keys < key_col) | ((keys == key_col) & (lane < sub))
    rank = jnp.sum(jnp.where(less, 1.0, 0.0), axis=1, keepdims=True)
    lane_f = lane.astype(F32)
    hit = rank == lane_f
    order_row = jnp.sum(jnp.where(hit, sub.astype(F32), 0.0), axis=0, keepdims=True)
    sorted_row = jnp.sum(jnp.where(hit, key_col, 0.0), axis=0, keepdims=True)
    same = (sorted_row == pltpu.roll(sorted_row, 1, 1)) & (lane_row > 0)
    before_row = jnp.where(same, lane_row - 1, rows)
    upto = jnp.sum(jnp.where(key_col <= lane_f, 1.0, 0.0), axis=0, keepdims=True)
    below = jnp.sum(jnp.where(key_col < lane_f, 1.0, 0.0), axis=0, keepdims=True)
    last_row = jnp.where(upto > below, upto - 1.0, float(rows))
    named_row = jnp.zeros((tall, 128), F32)
    named_col = jnp.zeros((tall, 128), F32)
    for i in range(half):
        named_row = named_row + jnp.where(lane == pair[0, i], 1.0, 0.0)
        named_col = named_col + jnp.where(sub == pair[0, i], 1.0, 0.0)
    free_row = (named_row == 0.0) & (lane < aggs)
    free_col = (named_col == 0.0) & (sub < aggs)
    rank_free = jnp.sum(jnp.where(free_row & (lane < sub), 1.0, 0.0), axis=1, keepdims=True)
    rest_row = jnp.sum(
        jnp.where(free_col & (rank_free == lane_f), sub.astype(F32), 0.0), axis=0, keepdims=True
    )
    tab_v[0:1, :] = order_row.astype(jnp.int32)
    tab_v[1:2, :] = before_row
    tab_v[2:3, :] = last_row.astype(jnp.int32)
    tab_v[3:4, :] = rest_row.astype(jnp.int32)
    tab_copy = pltpu.make_async_copy(tab_v, tab, tab_sem)
    tab_copy.start()

    run[rows] = jnp.zeros((width, width), F32)
    for i in range(a_chunks):
        a_copies[i].wait()

        def lay(r, _, i=i):
            row = i * a_rows + r
            a_cat[row] = jnp.concatenate([a_buf[row, n] for n in range(slots)], axis=1)
            p_t[row] = ext[rows + row].T
            return 0

        lax.fori_loop(0, a_rows, lay, 0, unroll=2)
    m_copy.wait()

    def turn(k, _):
        m_t[k] = m_buf[k].T
        return 0

    lax.fori_loop(0, aggs, turn, 0, unroll=2)
    tab_copy.wait()

    for side, there in ((0, has_previous), (1, has_next)):
        base = side * 2 * rows

        @pl.when(jnp.logical_not(there))
        def _():
            def clear(r, _):
                ext[base + r] = jnp.zeros((width, width), BF16)
                return 0

            lax.fori_loop(0, rows, clear, 0, unroll=2)

    for chunk in range(CHUNKS):
        for side, there in ((0, has_previous), (1, has_next)):
            base = side * 2 * rows + chunk * per

            @pl.when(there)
            def _():
                halo_copy(side, chunk).wait_recv()

                def open_row(r, _):
                    ext[base + r] = unfold(halo[side, chunk * per + r])
                    return 0

                lax.fori_loop(0, per, open_row, 0, unroll=2)

    def part_copy(q):
        owner = first + bucket_of[q]
        at_owner = slab - owner + REACH
        return pltpu.make_async_remote_copy(
            src_ref=send.at[q],
            dst_ref=recv.at[at_owner],
            send_sem=part_send.at[q],
            recv_sem=part_recv.at[at_owner],
            device_id=(owner, grp),
            device_id_type=MESH,
        )

    def row_step(k, _):
        r = jnp.clip(tab[0, k], 0, rows - 1)
        picked = jnp.concatenate([ext[nbr[r, n]] for n in range(slots)], axis=0)
        partial_w = jnp.dot(a_cat[r], picked, preferred_element_type=F32).astype(BF16)
        part = jnp.dot(p_t[r], partial_w, preferred_element_type=F32)
        run[k] = part + run[jnp.clip(tab[1, k], 0, rows)]
        return 0

    for q in range(WINDOW):
        begin, end = q * capacity, min((q + 1) * capacity, rows)
        lax.fori_loop(begin, end, row_step, 0, unroll=4)

        def gather(k, _, q=q):
            block = fold(run[jnp.clip(tab[2, q * aggs + k], 0, rows)])
            if q < REACH:
                send[q, k] = block.astype(BF16)
            else:
                acc[k] = block
            return 0

        lax.fori_loop(0, aggs, gather, 0, unroll=2)
        if q < REACH:
            part_copy(q).start()

    offsets = sorted((d for d in range(-REACH, REACH + 1) if d != 0), key=abs)
    for offset in offsets:
        at_here = offset + REACH

        @pl.when(sends_here(offset))
        def _():
            pltpu.make_async_remote_copy(
                src_ref=recv.at[at_here],
                dst_ref=recv.at[at_here],
                send_sem=part_send.at[0],
                recv_sem=part_recv.at[at_here],
                device_id=(slab, grp),
                device_id_type=MESH,
            ).wait_recv()
            acc[...] += recv[at_here].astype(F32)

    def open_sum(k, _):
        one_buf[k] = unfold(acc[k])
        return 0

    lax.fori_loop(0, aggs, open_sum, 0, unroll=2)
    one_copy = pltpu.make_async_copy(one_buf, one_hbm, out_sem.at[0])
    one_copy.start()

    def away(t, _):
        k = jnp.where(parity == 0, half + t, jnp.clip(tab[3, t], 0, aggs - 1))
        tx[t] = fold(galerkin(one_buf[k], m_t[k], m_buf[k])).astype(BF16)
        return 0

    lax.fori_loop(0, half, away, 0, unroll=half)
    pair_copy = pltpu.make_async_remote_copy(
        src_ref=tx, dst_ref=rx, send_sem=pair_send, recv_sem=pair_recv,
        device_id=(slab, grp_mate), device_id_type=MESH,
    )
    pair_copy.start()

    def home(t, _):
        k = jnp.where(parity == 0, t, pair[0, t])
        two_buf[t] = galerkin(one_buf[k], m_t[k], m_buf[k])
        return 0

    lax.fori_loop(0, half, home, 0, unroll=half)
    pair_copy.wait_recv()
    for t in range(half):
        before = sum((pair[0, i] < pair[0, t]).astype(jnp.int32) for i in range(half))
        at_rx = jnp.where(parity == 0, before, t)
        two_buf[t] += unfold(rx[at_rx].astype(F32))
    two_copy = pltpu.make_async_copy(two_buf, two_hbm, out_sem.at[1])
    two_copy.start()

    pair_copy.wait_send()
    for q in range(REACH):
        part_copy(q).wait_send()
    for chunk in range(CHUNKS):
        @pl.when(has_next)
        def _():
            halo_copy(0, chunk).wait_send()

        @pl.when(has_previous)
        def _():
            halo_copy(1, chunk).wait_send()
    one_copy.wait()
    two_copy.wait()


def on_device(n_slab, n_grp, a_blocks, neighbors, prolong, agg_ids, coarse_prolong, pairing):
    rows, slots, width, _ = a_blocks.shape
    aggs = coarse_prolong.shape[0]
    half = aggs // 2
    sizes = (n_slab, n_grp, rows, slots, width, aggs)
    a_chunks = 7
    dma = pltpu.SemaphoreType.DMA
    scratch = [
        pltpu.VMEM((rows, slots, width, width), BF16),
        pltpu.VMEM((rows, width, slots * width), BF16),
        pltpu.VMEM((3 * rows, width, width), BF16),
        pltpu.VMEM((rows, width // 2, 2 * width), BF16),
        pltpu.VMEM((2, rows, width // 2, 2 * width), BF16),
        pltpu.VMEM((rows, width, width), BF16),
        pltpu.VMEM((aggs, width, width), BF16),
        pltpu.VMEM((aggs, width, width), BF16),
        pltpu.VMEM((rows + 1, width, width), F32),
        pltpu.VMEM((REACH, aggs, width // 2, 2 * width), BF16),
        pltpu.VMEM((2 * REACH + 1, aggs, width // 2, 2 * width), BF16),
        pltpu.VMEM((aggs, width // 2, 2 * width), F32),
        pltpu.VMEM((aggs, width, width), F32),
        pltpu.VMEM((half, width, width), F32),
        pltpu.VMEM((half, width // 2, 2 * width), BF16),
        pltpu.VMEM((half, width // 2, 2 * width), BF16),
        pltpu.VMEM((8, 128), jnp.int32),
        pltpu.SMEM((8, 128), jnp.int32),
        dma((a_chunks,)),
        dma((2,)),
        dma,
        dma((2,)),
        dma((2, CHUNKS)),
        dma((2, CHUNKS)),
        dma((REACH,)),
        dma((2 * REACH + 1,)),
        dma,
        dma,
    ]
    smem = pl.BlockSpec(memory_space=pltpu.SMEM)
    vmem = pl.BlockSpec(memory_space=pltpu.VMEM)
    hbm = pl.BlockSpec(memory_space=pl.ANY)
    return pl.pallas_call(
        functools.partial(kernel, sizes),
        out_shape=(
            jax.ShapeDtypeStruct((aggs, width, width), F32),
            jax.ShapeDtypeStruct((half, width, width), F32),
        ),
        in_specs=[smem, vmem, smem, hbm, hbm, hbm],
        out_specs=(hbm, hbm),
        scratch_shapes=scratch,
        compiler_params=pltpu.CompilerParams(
            collective_id=0, has_side_effects=True, vmem_limit_bytes=56 * 2**20
        ),
    )(neighbors, agg_ids.reshape(1, rows), pairing, a_blocks, prolong, coarse_prolong)


def solution(mesh):
    placed = (
        P(("slab", "grp"), None, None, None),
        P(("slab", "grp"), None),
        P(("slab", "grp"), None, None),
        P(("slab", "grp")),
        P(("slab", "grp"), None, None),
        P(("slab", "grp"), None),
    )
    return jax.shard_map(
        functools.partial(on_device, mesh.shape["slab"], mesh.shape["grp"]),
        mesh=mesh,
        in_specs=placed,
        out_specs=(P(("slab", "grp"), None, None), P(("slab", "grp"), None, None)),
        check_vma=False,
    )
```

```python
import functools

import jax
import jax.numpy as jnp
from jax import lax
from jax.experimental import pallas as pl
from jax.experimental.pallas import tpu as pltpu
from jax.sharding import PartitionSpec as P

MESH = pl.DeviceIdType.MESH
WINDOW = 5
REACH = WINDOW - 1
CHUNKS = 4
F32 = jnp.float32
BF16 = jnp.bfloat16


def fold(block):
    half = block.shape[0] // 2
    return jnp.concatenate([block[:half], block[half:]], axis=1)


def unfold(block):
    width = block.shape[1] // 2
    return jnp.concatenate([block[:, :width], block[:, width:]], axis=0)


def galerkin(block, map_t, map_):
    high = block.astype(BF16)
    low = (block - high.astype(F32)).astype(BF16)
    inner = jnp.dot(map_t, high, preferred_element_type=F32) + jnp.dot(
        map_t, low, preferred_element_type=F32
    )
    high = inner.astype(BF16)
    low = (inner - high.astype(F32)).astype(BF16)
    return jnp.dot(high, map_, preferred_element_type=F32) + jnp.dot(
        low, map_, preferred_element_type=F32
    )


def kernel(
    sizes,
    nbr_hbm, agg_hbm, pair_hbm, a_hbm, p_hbm, m_hbm,
    acc, two,
    nbr, agg, pair, a_buf, a_cat, ext, p_fold, halo, p_t, m_buf, m_t, w_buf, run, send, recv, one_buf, tx, rx, tab_v, tab,
    a_sem, in_sem, tab_sem, halo_send, halo_recv, part_send, part_recv, pair_send, pair_recv,
):
    n_slab, n_grp, rows, slots, width, aggs = sizes
    half = aggs // 2
    capacity = (rows + WINDOW - 1) // WINDOW
    slab = lax.axis_index("slab")
    grp = lax.axis_index("grp")

    def window(s):
        return jnp.clip(s - WINDOW // 2, 0, n_slab - WINDOW)

    first = window(slab)
    chip_mate = slab + 1 - 2 * (slab % 2)
    grp_mate = grp + 1 - 2 * (grp % 2)
    parity = grp % 2

    p_copy = pltpu.make_async_copy(p_hbm, ext.at[pl.ds(rows, rows)], in_sem.at[0])
    p_copy.start()
    m_copy = pltpu.make_async_copy(m_hbm, m_buf, in_sem.at[1])
    small = [
        pltpu.make_async_copy(agg_hbm, agg, in_sem.at[2]),
        pltpu.make_async_copy(pair_hbm, pair, in_sem.at[3]),
        pltpu.make_async_copy(nbr_hbm, nbr, in_sem.at[4]),
    ]
    for copy in small:
        copy.start()
    a_chunks = a_sem.shape[0]
    a_rows = rows // a_chunks
    a_copies = [
        pltpu.make_async_copy(a_hbm.at[pl.ds(i * a_rows, a_rows)], a_buf.at[pl.ds(i * a_rows, a_rows)], a_sem.at[i])
        for i in range(a_chunks)
    ]
    for copy in a_copies:
        copy.start()
    m_copy.start()

    barrier = pltpu.get_barrier_semaphore()

    def sends_here(offset):
        source = slab + offset
        low = window(source)
        return (source >= 0) & (source < n_slab) & (low <= slab) & (slab < low + WINDOW)

    for offset in range(-REACH, REACH + 1):
        if offset != 0:
            @pl.when(sends_here(offset))
            def _():
                pl.semaphore_signal(barrier, inc=1, device_id=(slab + offset, grp), device_id_type=MESH)
    pl.semaphore_signal(barrier, inc=1, device_id=(slab, grp_mate), device_id_type=MESH)

    p_copy.wait()
    per = rows // CHUNKS

    def halo_copy(side, chunk):
        span = pl.ds(chunk * per, per)
        target = slab + 1 - 2 * side
        return pltpu.make_async_remote_copy(
            src_ref=p_fold.at[span],
            dst_ref=halo.at[side, span],
            send_sem=halo_send.at[side, chunk],
            recv_sem=halo_recv.at[side, chunk],
            device_id=(target, grp),
            device_id_type=MESH,
        )

    has_next = slab < n_slab - 1
    has_previous = slab > 0
    for chunk in range(CHUNKS):
        def fold_row(r, _, chunk=chunk):
            p_fold[chunk * per + r] = fold(ext[rows + chunk * per + r])
            return 0

        lax.fori_loop(0, per, fold_row, 0, unroll=per)
        if chunk == 0:
            pl.semaphore_wait(barrier, WINDOW)

        @pl.when(has_next)
        def _():
            halo_copy(0, chunk).start()

        @pl.when(has_previous)
        def _():
            halo_copy(1, chunk).start()

    tag = []
    for j in range(WINDOW):
        owner = first + j
        kind = jnp.where(owner == slab, 2, jnp.where(owner == chip_mate, 1, 0))
        tag.append(kind * WINDOW + j)
    place = [sum((tag[i] < tag[j]).astype(jnp.int32) for i in range(WINDOW)) for j in range(WINDOW)]
    bucket_of = [
        sum(jnp.where(place[j] == q, j, 0) for j in range(WINDOW)) for q in range(WINDOW)
    ]
    tall = 64
    sub = lax.broadcasted_iota(jnp.int32, (tall, 128), 0)
    lane = lax.broadcasted_iota(jnp.int32, (tall, 128), 1)
    lane_row = lax.broadcasted_iota(jnp.int32, (1, 128), 1)
    tab_v[...] = jnp.zeros_like(tab_v)
    for copy in small:
        copy.wait()
    tab_v[0:1, 0:rows] = agg[...]
    ids = tab_v[0:1, :]
    owner_row = lax.div(ids, jnp.int32(n_grp * aggs))
    inside = lax.rem(ids, jnp.int32(aggs))
    bucket = owner_row - first
    at = jnp.zeros_like(bucket)
    for j in range(WINDOW):
        at = at + jnp.where(bucket == j, place[j], 0)
    far = 1000
    key_row = jnp.where(lane_row < rows, at * aggs + inside, far).astype(F32)
    keys = jnp.broadcast_to(key_row, (tall, 128))
    key_col = jnp.sum(jnp.where(sub == lane, keys, 0.0), axis=1, keepdims=True)
    less = (keys < key_col) | ((keys == key_col) & (lane < sub))
    rank = jnp.sum(jnp.where(less, 1.0, 0.0), axis=1, keepdims=True)
    lane_f = lane.astype(F32)
    hit = rank == lane_f
    order_row = jnp.sum(jnp.where(hit, sub.astype(F32), 0.0), axis=0, keepdims=True)
    sorted_row = jnp.sum(jnp.where(hit, key_col, 0.0), axis=0, keepdims=True)
    same = (sorted_row == pltpu.roll(sorted_row, 1, 1)) & (lane_row > 0)
    before_row = jnp.where(same, lane_row - 1, rows)
    upto = jnp.sum(jnp.where(key_col <= lane_f, 1.0, 0.0), axis=0, keepdims=True)
    below = jnp.sum(jnp.where(key_col < lane_f, 1.0, 0.0), axis=0, keepdims=True)
    last_row = jnp.where(upto > below, upto - 1.0, float(rows))
    named_row = jnp.zeros((tall, 128), F32)
    named_col = jnp.zeros((tall, 128), F32)
    for i in range(half):
        named_row = named_row + jnp.where(lane == pair[0, i], 1.0, 0.0)
        named_col = named_col + jnp.where(sub == pair[0, i], 1.0, 0.0)
    free_row = (named_row == 0.0) & (lane < aggs)
    free_col = (named_col == 0.0) & (sub < aggs)
    rank_free = jnp.sum(jnp.where(free_row & (lane < sub), 1.0, 0.0), axis=1, keepdims=True)
    rest_row = jnp.sum(
        jnp.where(free_col & (rank_free == lane_f), sub.astype(F32), 0.0), axis=0, keepdims=True
    )
    tab_v[0:1, :] = order_row.astype(jnp.int32)
    tab_v[1:2, :] = before_row
    tab_v[2:3, :] = last_row.astype(jnp.int32)
    tab_v[3:4, :] = rest_row.astype(jnp.int32)
    tab_copy = pltpu.make_async_copy(tab_v, tab, tab_sem)
    tab_copy.start()

    run[rows] = jnp.zeros((width, width), F32)
    for i in range(a_chunks):
        a_copies[i].wait()

        def lay(r, _, i=i):
            row = i * a_rows + r
            a_cat[row] = jnp.concatenate([a_buf[row, n] for n in range(slots)], axis=1)
            p_t[row] = ext[rows + row].T
            return 0

        lax.fori_loop(0, a_rows, lay, 0, unroll=a_rows)
    m_copy.wait()

    def turn(k, _):
        m_t[k] = m_buf[k].T
        return 0

    lax.fori_loop(0, aggs, turn, 0, unroll=half)
    tab_copy.wait()

    for side, there in ((0, has_previous), (1, has_next)):
        base = side * 2 * rows

        @pl.when(jnp.logical_not(there))
        def _():
            def clear(r, _):
                ext[base + r] = jnp.zeros((width, width), BF16)
                return 0

            lax.fori_loop(0, rows, clear, 0, unroll=2)

    for chunk in range(CHUNKS):
        for side, there in ((0, has_previous), (1, has_next)):
            base = side * 2 * rows + chunk * per

            @pl.when(there)
            def _():
                halo_copy(side, chunk).wait_recv()

                def open_row(r, _):
                    ext[base + r] = unfold(halo[side, chunk * per + r])
                    return 0

                lax.fori_loop(0, per, open_row, 0, unroll=per)

    def part_copy(q):
        owner = first + bucket_of[q]
        at_owner = slab - owner + REACH
        return pltpu.make_async_remote_copy(
            src_ref=send.at[q],
            dst_ref=recv.at[at_owner],
            send_sem=part_send.at[q],
            recv_sem=part_recv.at[at_owner],
            device_id=(owner, grp),
            device_id_type=MESH,
        )

    def row_at(k):
        return jnp.clip(tab[0, k], 0, rows - 1)

    def weigh(k, _):
        r = row_at(k)
        picked = jnp.concatenate(
            [ext[jnp.clip(nbr[n, r], 0, 3 * rows - 1)] for n in range(slots)], axis=0
        )
        w_buf[k] = jnp.dot(a_cat[r], picked, preferred_element_type=F32).astype(BF16)
        return 0

    def project(k, _):
        part = jnp.dot(p_t[row_at(k)], w_buf[k], preferred_element_type=F32)
        run[k] = part + run[jnp.clip(tab[1, k], 0, rows)]
        return 0

    for q in range(WINDOW):
        begin, end = q * capacity, min((q + 1) * capacity, rows)
        lax.fori_loop(begin, end, weigh, 0, unroll=end - begin)
        lax.fori_loop(begin, end, project, 0, unroll=end - begin)

        def gather(k, _, q=q):
            block = fold(run[jnp.clip(tab[2, q * aggs + k], 0, rows)])
            if q < REACH:
                send[q, k] = block.astype(BF16)
            else:
                acc[k] = block
            return 0

        lax.fori_loop(0, aggs, gather, 0, unroll=aggs)
        if q < REACH:
            part_copy(q).start()

    offsets = sorted((d for d in range(-REACH, REACH + 1) if d != 0), key=abs)
    for offset in offsets:
        at_here = offset + REACH

        @pl.when(sends_here(offset))
        def _():
            pltpu.make_async_remote_copy(
                src_ref=recv.at[at_here],
                dst_ref=recv.at[at_here],
                send_sem=part_send.at[0],
                recv_sem=part_recv.at[at_here],
                device_id=(slab, grp),
                device_id_type=MESH,
            ).wait_recv()
            acc[...] += recv[at_here].astype(F32)

    def open_sum(k, _):
        one_buf[k] = unfold(acc[k])
        return 0

    lax.fori_loop(0, aggs, open_sum, 0, unroll=aggs)

    def away(t, _):
        k = jnp.where(parity == 0, half + t, jnp.clip(tab[3, t], 0, aggs - 1))
        tx[t] = fold(galerkin(one_buf[k], m_t[k], m_buf[k])).astype(BF16)
        return 0

    lax.fori_loop(0, half, away, 0, unroll=half)
    pair_copy = pltpu.make_async_remote_copy(
        src_ref=tx, dst_ref=rx, send_sem=pair_send, recv_sem=pair_recv,
        device_id=(slab, grp_mate), device_id_type=MESH,
    )
    pair_copy.start()

    def home(t, _):
        k = jnp.where(parity == 0, t, jnp.clip(pair[0, t], 0, aggs - 1))
        two[t] = fold(galerkin(one_buf[k], m_t[k], m_buf[k]))
        return 0

    lax.fori_loop(0, half, home, 0, unroll=half)
    pair_copy.wait_recv()
    for t in range(half):
        before = sum((pair[0, i] < pair[0, t]).astype(jnp.int32) for i in range(half))
        at_rx = jnp.where(parity == 0, before, t)
        two[t] += rx[at_rx].astype(F32)

    pair_copy.wait_send()
    for q in range(REACH):
        part_copy(q).wait_send()
    for chunk in range(CHUNKS):
        @pl.when(has_next)
        def _():
            halo_copy(0, chunk).wait_send()

        @pl.when(has_previous)
        def _():
            halo_copy(1, chunk).wait_send()


def spread(acc, two_folded, one_hbm, two_hbm, one_buf, two_buf, sem):
    for k in range(acc.shape[0]):
        one_buf[k] = unfold(acc[k])
    one_copy = pltpu.make_async_copy(one_buf, one_hbm, sem.at[0])
    one_copy.start()
    for k in range(two_folded.shape[0]):
        two_buf[k] = unfold(two_folded[k])
    two_copy = pltpu.make_async_copy(two_buf, two_hbm, sem.at[1])
    two_copy.start()
    one_copy.wait()
    two_copy.wait()


def on_device(n_slab, n_grp, a_blocks, neighbors, prolong, agg_ids, coarse_prolong, pairing):
    rows, slots, width, _ = a_blocks.shape
    aggs = coarse_prolong.shape[0]
    half = aggs // 2
    sizes = (n_slab, n_grp, rows, slots, width, aggs)
    a_chunks = 7
    dma = pltpu.SemaphoreType.DMA
    scratch = [
        pltpu.SMEM((slots, rows), jnp.int32),
        pltpu.VMEM((1, rows), jnp.int32),
        pltpu.SMEM((1, half), jnp.int32),
        pltpu.VMEM((rows, slots, width, width), BF16),
        pltpu.VMEM((rows, width, slots * width), BF16),
        pltpu.VMEM((3 * rows, width, width), BF16),
        pltpu.VMEM((rows, width // 2, 2 * width), BF16),
        pltpu.VMEM((2, rows, width // 2, 2 * width), BF16),
        pltpu.VMEM((rows, width, width), BF16),
        pltpu.VMEM((aggs, width, width), BF16),
        pltpu.VMEM((aggs, width, width), BF16),
        pltpu.VMEM((rows, width, width), BF16),
        pltpu.VMEM((rows + 1, width, width), F32),
        pltpu.VMEM((REACH, aggs, width // 2, 2 * width), BF16),
        pltpu.VMEM((2 * REACH + 1, aggs, width // 2, 2 * width), BF16),
        pltpu.VMEM((aggs, width, width), F32),
        pltpu.VMEM((half, width // 2, 2 * width), BF16),
        pltpu.VMEM((half, width // 2, 2 * width), BF16),
        pltpu.VMEM((8, 128), jnp.int32),
        pltpu.SMEM((8, 128), jnp.int32),
        dma((a_chunks,)),
        dma((5,)),
        dma,
        dma((2, CHUNKS)),
        dma((2, CHUNKS)),
        dma((REACH,)),
        dma((2 * REACH + 1,)),
        dma,
        dma,
    ]
    vmem = pl.BlockSpec(memory_space=pltpu.VMEM)
    hbm = pl.BlockSpec(memory_space=pltpu.HBM)
    folded = pl.pallas_call(
        functools.partial(kernel, sizes),
        out_shape=(
            jax.ShapeDtypeStruct((aggs, width // 2, 2 * width), F32),
            jax.ShapeDtypeStruct((half, width // 2, 2 * width), F32),
        ),
        in_specs=[hbm] * 6,
        out_specs=(vmem, vmem),
        scratch_shapes=scratch,
        compiler_params=pltpu.CompilerParams(
            collective_id=0, has_side_effects=True, vmem_limit_bytes=30 * 2**20
        ),
    )(*(pltpu.with_memory_space_constraint(x, pltpu.HBM) for x in (neighbors.T, agg_ids.reshape(1, rows), pairing, a_blocks, prolong, coarse_prolong)))
    return pl.pallas_call(
        spread,
        out_shape=(
            jax.ShapeDtypeStruct((aggs, width, width), F32),
            jax.ShapeDtypeStruct((half, width, width), F32),
        ),
        in_specs=[vmem, vmem],
        out_specs=(hbm, hbm),
        scratch_shapes=[
            pltpu.VMEM((aggs, width, width), F32),
            pltpu.VMEM((half, width, width), F32),
            dma((2,)),
        ],
        compiler_params=pltpu.CompilerParams(vmem_limit_bytes=4 * 2**20),
    )(*folded)


def solution(mesh):
    placed = (
        P(("slab", "grp"), None, None, None),
        P(("slab", "grp"), None),
        P(("slab", "grp"), None, None),
        P(("slab", "grp")),
        P(("slab", "grp"), None, None),
        P(("slab", "grp"), None),
    )
    return jax.shard_map(
        functools.partial(on_device, mesh.shape["slab"], mesh.shape["grp"]),
        mesh=mesh,
        in_specs=placed,
        out_specs=(P(("slab", "grp"), None, None), P(("slab", "grp"), None, None)),
        check_vma=False,
    )
```

```python
import functools

import jax
import jax.numpy as jnp
from jax import lax
from jax.experimental import pallas as pl
from jax.experimental.pallas import tpu as pltpu
from jax.sharding import PartitionSpec as P

MESH = pl.DeviceIdType.MESH
WINDOW = 5
REACH = WINDOW - 1
HANDED, SHARED = 1, 2
OFFSETS = (-1, 1, -2, 2, -4, 4)
CHUNKS = 4
F32 = jnp.float32
BF16 = jnp.bfloat16


def fold(block):
    half = block.shape[0] // 2
    return jnp.concatenate([block[:half], block[half:]], axis=1)


def unfold(block):
    width = block.shape[1] // 2
    return jnp.concatenate([block[:, :width], block[:, width:]], axis=0)


def galerkin(block, map_t, map_):
    high = block.astype(BF16)
    low = (block - high.astype(F32)).astype(BF16)
    inner = jnp.dot(map_t, high, preferred_element_type=F32) + jnp.dot(
        map_t, low, preferred_element_type=F32
    )
    high = inner.astype(BF16)
    low = (inner - high.astype(F32)).astype(BF16)
    return jnp.dot(high, map_, preferred_element_type=F32) + jnp.dot(
        low, map_, preferred_element_type=F32
    )


def kernel(
    sizes,
    nbr_hbm, agg_hbm, pair_hbm, a_hbm, p_hbm, m_hbm,
    acc, two,
    nbr, agg, pair, a_buf, a_cat, ext, p_fold, halo, p_t, m_buf, m_t, w_buf, run, send, recv, hand, handed, one_buf, tx, rx, tab_v, tab,
    a_sem, p_sem, in_sem, tab_sem, halo_send, halo_recv, part_send, part_recv, hand_recv, pair_send, pair_recv,
):
    n_slab, n_grp, rows, slots, width, aggs = sizes
    half = aggs // 2
    capacity = (rows + WINDOW - 1) // WINDOW
    slab = lax.axis_index("slab")
    grp = lax.axis_index("grp")

    def owners(s):
        odd = s % 2
        side = 1 - 2 * odd
        low, high = s < 2, s >= n_slab - 2
        end = low | high
        direct = jnp.where(low, 2, jnp.where(high, n_slab - 3, s - 2 * side))
        far = jnp.where(low, 4, n_slab - 5)
        near = jnp.where(low, 3, n_slab - 4)
        outer = jnp.where(low, odd == 0, odd == 1)
        handed = jnp.where(end, jnp.where(outer, near, far), s + 2 * side)
        shared = jnp.where(end, jnp.where(outer, far, near), s - side)
        return direct, handed, shared, s + side, s

    owner_of = owners(slab)
    chip_mate = owner_of[3]
    grp_mate = grp + 1 - 2 * (grp % 2)
    parity = grp % 2

    per = rows // CHUNKS
    p_copies = [
        pltpu.make_async_copy(
            p_hbm.at[pl.ds(i * per, per)], ext.at[pl.ds(rows + i * per, per)], p_sem.at[i]
        )
        for i in range(CHUNKS)
    ]
    for copy in p_copies:
        copy.start()
    m_copy = pltpu.make_async_copy(m_hbm, m_buf, in_sem.at[1])
    small = [
        pltpu.make_async_copy(agg_hbm, agg, in_sem.at[2]),
        pltpu.make_async_copy(pair_hbm, pair, in_sem.at[3]),
        pltpu.make_async_copy(nbr_hbm, nbr, in_sem.at[4]),
    ]
    for copy in small:
        copy.start()
    a_chunks = a_sem.shape[0]
    a_rows = rows // a_chunks
    a_copies = [
        pltpu.make_async_copy(a_hbm.at[pl.ds(i * a_rows, a_rows)], a_buf.at[pl.ds(i * a_rows, a_rows)], a_sem.at[i])
        for i in range(a_chunks)
    ]
    for copy in a_copies:
        copy.start()
    m_copy.start()

    barrier = pltpu.get_barrier_semaphore()

    def sends_here(offset):
        source = slab + offset
        direct, _, shared, mate, _ = owners(source)
        return (source >= 0) & (source < n_slab) & ((direct == slab) | (shared == slab) | (mate == slab))

    senders = {offset: sends_here(offset) for offset in OFFSETS}
    for offset in OFFSETS:
        @pl.when(senders[offset])
        def _():
            pl.semaphore_signal(barrier, inc=1, device_id=(slab + offset, grp), device_id_type=MESH)
    pl.semaphore_signal(barrier, inc=1, device_id=(slab, grp_mate), device_id_type=MESH)

    def halo_copy(side, chunk):
        span = pl.ds(chunk * per, per)
        target = slab + 1 - 2 * side
        return pltpu.make_async_remote_copy(
            src_ref=p_fold.at[span],
            dst_ref=halo.at[side, span],
            send_sem=halo_send.at[side, chunk],
            recv_sem=halo_recv.at[side, chunk],
            device_id=(target, grp),
            device_id_type=MESH,
        )

    has_next = slab < n_slab - 1
    has_previous = slab > 0
    for chunk in range(CHUNKS):
        p_copies[chunk].wait()

        def fold_row(r, _, chunk=chunk):
            p_fold[chunk * per + r] = fold(ext[rows + chunk * per + r])
            return 0

        lax.fori_loop(0, per, fold_row, 0, unroll=per)
        if chunk == 0:
            pl.semaphore_wait(barrier, 4)

        @pl.when(has_next)
        def _():
            halo_copy(0, chunk).start()

        @pl.when(has_previous)
        def _():
            halo_copy(1, chunk).start()

    tall = 64
    sub = lax.broadcasted_iota(jnp.int32, (tall, 128), 0)
    lane = lax.broadcasted_iota(jnp.int32, (tall, 128), 1)
    lane_row = lax.broadcasted_iota(jnp.int32, (1, 128), 1)
    tab_v[...] = jnp.zeros_like(tab_v)
    for copy in small:
        copy.wait()
    tab_v[0:1, 0:rows] = agg[...]
    ids = tab_v[0:1, :]
    owner_row = lax.div(ids, jnp.int32(n_grp * aggs))
    inside = lax.rem(ids, jnp.int32(aggs))
    at = jnp.zeros_like(owner_row)
    for q in range(WINDOW):
        at = at + jnp.where(owner_row == owner_of[q], q, 0)
    far = 1000
    key_row = jnp.where(lane_row < rows, at * aggs + inside, far).astype(F32)
    keys = jnp.broadcast_to(key_row, (tall, 128))
    key_col = jnp.sum(jnp.where(sub == lane, keys, 0.0), axis=1, keepdims=True)
    less = (keys < key_col) | ((keys == key_col) & (lane < sub))
    rank = jnp.sum(jnp.where(less, 1.0, 0.0), axis=1, keepdims=True)
    lane_f = lane.astype(F32)
    hit = rank == lane_f
    order_row = jnp.sum(jnp.where(hit, sub.astype(F32), 0.0), axis=0, keepdims=True)
    sorted_row = jnp.sum(jnp.where(hit, key_col, 0.0), axis=0, keepdims=True)
    same = (sorted_row == pltpu.roll(sorted_row, 1, 1)) & (lane_row > 0)
    before_row = jnp.where(same, lane_row - 1, rows)
    upto = jnp.sum(jnp.where(key_col <= lane_f, 1.0, 0.0), axis=0, keepdims=True)
    below = jnp.sum(jnp.where(key_col < lane_f, 1.0, 0.0), axis=0, keepdims=True)
    last_row = jnp.where(upto > below, upto - 1.0, float(rows))
    named_row = jnp.zeros((tall, 128), F32)
    named_col = jnp.zeros((tall, 128), F32)
    for i in range(half):
        named_row = named_row + jnp.where(lane == pair[0, i], 1.0, 0.0)
        named_col = named_col + jnp.where(sub == pair[0, i], 1.0, 0.0)
    free_row = (named_row == 0.0) & (lane < aggs)
    free_col = (named_col == 0.0) & (sub < aggs)
    rank_free = jnp.sum(jnp.where(free_row & (lane < sub), 1.0, 0.0), axis=1, keepdims=True)
    rest_row = jnp.sum(
        jnp.where(free_col & (rank_free == lane_f), sub.astype(F32), 0.0), axis=0, keepdims=True
    )
    tab_v[0:1, :] = order_row.astype(jnp.int32)
    tab_v[1:2, :] = before_row
    tab_v[2:3, :] = last_row.astype(jnp.int32)
    tab_v[3:4, :] = rest_row.astype(jnp.int32)
    tab_copy = pltpu.make_async_copy(tab_v, tab, tab_sem)
    tab_copy.start()

    run[rows] = jnp.zeros((width, width), F32)
    for i in range(a_chunks):
        a_copies[i].wait()

        def lay(r, _, i=i):
            row = i * a_rows + r
            a_cat[row] = jnp.concatenate([a_buf[row, n] for n in range(slots)], axis=1)
            p_t[row] = ext[rows + row].T
            return 0

        lax.fori_loop(0, a_rows, lay, 0, unroll=a_rows)
    m_copy.wait()

    def turn(k, _):
        m_t[k] = m_buf[k].T
        return 0

    lax.fori_loop(0, aggs, turn, 0, unroll=half)
    tab_copy.wait()

    for side, there in ((0, has_previous), (1, has_next)):
        base = side * 2 * rows

        @pl.when(jnp.logical_not(there))
        def _():
            def clear(r, _):
                ext[base + r] = jnp.zeros((width, width), BF16)
                return 0

            lax.fori_loop(0, rows, clear, 0, unroll=2)

    for chunk in range(CHUNKS):
        for side, there in ((0, has_previous), (1, has_next)):
            base = side * 2 * rows + chunk * per

            @pl.when(there)
            def _():
                halo_copy(side, chunk).wait_recv()

                def open_row(r, _):
                    ext[base + r] = unfold(halo[side, chunk * per + r])
                    return 0

                lax.fori_loop(0, per, open_row, 0, unroll=per)

    def part_copy(q):
        owner = owner_of[q]
        at_owner = slab - owner + REACH
        if q == HANDED:
            source, target, arrived = hand, handed, hand_recv
        else:
            source, target, arrived = send.at[q], recv.at[at_owner], part_recv.at[at_owner]
        return pltpu.make_async_remote_copy(
            src_ref=source,
            dst_ref=target,
            send_sem=part_send.at[q],
            recv_sem=arrived,
            device_id=(chip_mate if q == HANDED else owner, grp),
            device_id_type=MESH,
        )

    def row_at(k):
        return jnp.clip(tab[0, k], 0, rows - 1)

    def weigh(k, _):
        r = row_at(k)
        picked = jnp.concatenate(
            [ext[jnp.clip(nbr[n, r], 0, 3 * rows - 1)] for n in range(slots)], axis=0
        )
        w_buf[k] = jnp.dot(a_cat[r], picked, preferred_element_type=F32).astype(BF16)
        return 0

    def project(k, _):
        part = jnp.dot(p_t[row_at(k)], w_buf[k], preferred_element_type=F32)
        run[k] = part + run[jnp.clip(tab[1, k], 0, rows)]
        return 0

    for q in range(WINDOW):
        begin, end = q * capacity, min((q + 1) * capacity, rows)
        lax.fori_loop(begin, end, weigh, 0, unroll=end - begin)
        lax.fori_loop(begin, end, project, 0, unroll=end - begin)

        def gather(k, _, q=q):
            block = fold(run[jnp.clip(tab[2, q * aggs + k], 0, rows)])
            if q == HANDED:
                hand[k] = block
            elif q == SHARED:
                send[q, k] = (block + handed[k]).astype(BF16)
            elif q < REACH:
                send[q, k] = block.astype(BF16)
            else:
                acc[k] = block
            return 0

        if q == SHARED:
            part_copy(HANDED).wait_recv()

        lax.fori_loop(0, aggs, gather, 0, unroll=aggs)
        if q < REACH:
            part_copy(q).start()

    for offset in OFFSETS:
        at_here = offset + REACH

        @pl.when(senders[offset])
        def _():
            pltpu.make_async_remote_copy(
                src_ref=recv.at[at_here],
                dst_ref=recv.at[at_here],
                send_sem=part_send.at[0],
                recv_sem=part_recv.at[at_here],
                device_id=(slab, grp),
                device_id_type=MESH,
            ).wait_recv()
            acc[...] += recv[at_here].astype(F32)

    def open_sum(k, _):
        one_buf[k] = unfold(acc[k])
        return 0

    lax.fori_loop(0, aggs, open_sum, 0, unroll=aggs)

    def away(t, _):
        k = jnp.where(parity == 0, half + t, jnp.clip(tab[3, t], 0, aggs - 1))
        tx[t] = fold(galerkin(one_buf[k], m_t[k], m_buf[k])).astype(BF16)
        return 0

    lax.fori_loop(0, half, away, 0, unroll=half)
    pair_copy = pltpu.make_async_remote_copy(
        src_ref=tx, dst_ref=rx, send_sem=pair_send, recv_sem=pair_recv,
        device_id=(slab, grp_mate), device_id_type=MESH,
    )
    pair_copy.start()

    def home(t, _):
        k = jnp.where(parity == 0, t, jnp.clip(pair[0, t], 0, aggs - 1))
        two[t] = fold(galerkin(one_buf[k], m_t[k], m_buf[k]))
        return 0

    lax.fori_loop(0, half, home, 0, unroll=half)
    pair_copy.wait_recv()
    for t in range(half):
        before = sum((pair[0, i] < pair[0, t]).astype(jnp.int32) for i in range(half))
        at_rx = jnp.where(parity == 0, before, t)
        two[t] += rx[at_rx].astype(F32)

    pair_copy.wait_send()
    for q in range(REACH):
        part_copy(q).wait_send()
    for chunk in range(CHUNKS):
        @pl.when(has_next)
        def _():
            halo_copy(0, chunk).wait_send()

        @pl.when(has_previous)
        def _():
            halo_copy(1, chunk).wait_send()


def spread(acc, two_folded, one_hbm, two_hbm, one_buf, two_buf, sem):
    for k in range(acc.shape[0]):
        one_buf[k] = unfold(acc[k])
    one_copy = pltpu.make_async_copy(one_buf, one_hbm, sem.at[0])
    one_copy.start()
    for k in range(two_folded.shape[0]):
        two_buf[k] = unfold(two_folded[k])
    two_copy = pltpu.make_async_copy(two_buf, two_hbm, sem.at[1])
    two_copy.start()
    one_copy.wait()
    two_copy.wait()


def on_device(n_slab, n_grp, a_blocks, neighbors, prolong, agg_ids, coarse_prolong, pairing):
    rows, slots, width, _ = a_blocks.shape
    aggs = coarse_prolong.shape[0]
    half = aggs // 2
    sizes = (n_slab, n_grp, rows, slots, width, aggs)
    a_chunks = 7
    dma = pltpu.SemaphoreType.DMA
    scratch = [
        pltpu.SMEM((slots, rows), jnp.int32),
        pltpu.VMEM((1, rows), jnp.int32),
        pltpu.SMEM((1, half), jnp.int32),
        pltpu.VMEM((rows, slots, width, width), BF16),
        pltpu.VMEM((rows, width, slots * width), BF16),
        pltpu.VMEM((3 * rows, width, width), BF16),
        pltpu.VMEM((rows, width // 2, 2 * width), BF16),
        pltpu.VMEM((2, rows, width // 2, 2 * width), BF16),
        pltpu.VMEM((rows, width, width), BF16),
        pltpu.VMEM((aggs, width, width), BF16),
        pltpu.VMEM((aggs, width, width), BF16),
        pltpu.VMEM((rows, width, width), BF16),
        pltpu.VMEM((rows + 1, width, width), F32),
        pltpu.VMEM((REACH, aggs, width // 2, 2 * width), BF16),
        pltpu.VMEM((2 * REACH + 1, aggs, width // 2, 2 * width), BF16),
        pltpu.VMEM((aggs, width // 2, 2 * width), F32),
        pltpu.VMEM((aggs, width // 2, 2 * width), F32),
        pltpu.VMEM((aggs, width, width), F32),
        pltpu.VMEM((half, width // 2, 2 * width), BF16),
        pltpu.VMEM((half, width // 2, 2 * width), BF16),
        pltpu.VMEM((8, 128), jnp.int32),
        pltpu.SMEM((8, 128), jnp.int32),
        dma((a_chunks,)),
        dma((CHUNKS,)),
        dma((5,)),
        dma,
        dma((2, CHUNKS)),
        dma((2, CHUNKS)),
        dma((REACH,)),
        dma((2 * REACH + 1,)),
        dma,
        dma,
        dma,
    ]
    vmem = pl.BlockSpec(memory_space=pltpu.VMEM)
    hbm = pl.BlockSpec(memory_space=pltpu.HBM)
    folded = pl.pallas_call(
        functools.partial(kernel, sizes),
        out_shape=(
            jax.ShapeDtypeStruct((aggs, width // 2, 2 * width), F32),
            jax.ShapeDtypeStruct((half, width // 2, 2 * width), F32),
        ),
        in_specs=[hbm] * 6,
        out_specs=(vmem, vmem),
        scratch_shapes=scratch,
        compiler_params=pltpu.CompilerParams(
            collective_id=0, has_side_effects=True, vmem_limit_bytes=30 * 2**20
        ),
    )(*(pltpu.with_memory_space_constraint(x, pltpu.HBM) for x in (neighbors.T, agg_ids.reshape(1, rows), pairing, a_blocks, prolong, coarse_prolong)))
    return pl.pallas_call(
        spread,
        out_shape=(
            jax.ShapeDtypeStruct((aggs, width, width), F32),
            jax.ShapeDtypeStruct((half, width, width), F32),
        ),
        in_specs=[vmem, vmem],
        out_specs=(hbm, hbm),
        scratch_shapes=[
            pltpu.VMEM((aggs, width, width), F32),
            pltpu.VMEM((half, width, width), F32),
            dma((2,)),
        ],
        compiler_params=pltpu.CompilerParams(vmem_limit_bytes=4 * 2**20),
    )(*folded)


def solution(mesh):
    placed = (
        P(("slab", "grp"), None, None, None),
        P(("slab", "grp"), None),
        P(("slab", "grp"), None, None),
        P(("slab", "grp")),
        P(("slab", "grp"), None, None),
        P(("slab", "grp"), None),
    )
    return jax.shard_map(
        functools.partial(on_device, mesh.shape["slab"], mesh.shape["grp"]),
        mesh=mesh,
        in_specs=placed,
        out_specs=(P(("slab", "grp"), None, None), P(("slab", "grp"), None, None)),
        check_vma=False,
    )
```

```python
import functools

import jax
import jax.numpy as jnp
from jax import lax
from jax.experimental import pallas as pl
from jax.experimental.pallas import tpu as pltpu
from jax.sharding import PartitionSpec as P

MESH = pl.DeviceIdType.MESH
WINDOW = 5
REACH = WINDOW - 1
HANDED, SHARED = 1, 2
OFFSETS = (4, 2, 1, -1, -2, -4)
CHUNKS = 4
F32 = jnp.float32
BF16 = jnp.bfloat16


def fold(block):
    half = block.shape[0] // 2
    return jnp.concatenate([block[:half], block[half:]], axis=1)


def unfold(block):
    width = block.shape[1] // 2
    return jnp.concatenate([block[:, :width], block[:, width:]], axis=0)


def galerkin(block, map_t, map_):
    high = block.astype(BF16)
    low = (block - high.astype(F32)).astype(BF16)
    inner = jnp.dot(map_t, high, preferred_element_type=F32) + jnp.dot(
        map_t, low, preferred_element_type=F32
    )
    high = inner.astype(BF16)
    low = (inner - high.astype(F32)).astype(BF16)
    return jnp.dot(high, map_, preferred_element_type=F32) + jnp.dot(
        low, map_, preferred_element_type=F32
    )


def kernel(
    sizes,
    nbr_hbm, agg_hbm, pair_hbm, a_hbm, p_hbm, m_hbm,
    acc, two,
    nbr, agg, pair, a_buf, a_cat, ext, p_fold, halo, p_t, m_buf, m_t, w_buf, run, send, recv, hand, handed, one_buf, tx, rx, tab_v, tab,
    a_sem, p_sem, in_sem, tab_sem, halo_send, halo_recv, part_send, part_recv, hand_recv, pair_send, pair_recv,
):
    n_slab, n_grp, rows, slots, width, aggs = sizes
    half = aggs // 2
    capacity = (rows + WINDOW - 1) // WINDOW
    slab = lax.axis_index("slab")
    grp = lax.axis_index("grp")

    def owners(s):
        odd = s % 2
        side = 1 - 2 * odd
        low, high = s < 2, s >= n_slab - 2
        end = low | high
        direct = jnp.where(low, 2, jnp.where(high, n_slab - 3, s - 2 * side))
        far = jnp.where(low, 4, n_slab - 5)
        near = jnp.where(low, 3, n_slab - 4)
        outer = jnp.where(low, odd == 0, odd == 1)
        handed = jnp.where(end, jnp.where(outer, near, far), s + 2 * side)
        shared = jnp.where(end, jnp.where(outer, far, near), s - side)
        return direct, handed, shared, s + side, s

    owner_of = owners(slab)
    chip_mate = owner_of[3]
    grp_mate = grp + 1 - 2 * (grp % 2)
    parity = grp % 2

    barrier = pltpu.get_barrier_semaphore()

    def sends_here(offset):
        source = slab + offset
        direct, _, shared, mate, _ = owners(source)
        return (source >= 0) & (source < n_slab) & ((direct == slab) | (shared == slab) | (mate == slab))

    def greets(offset):
        source = slab + offset
        direct, _, shared, mate, _ = owners(source)
        end = (source < 2) | (source >= n_slab - 2)
        return (source >= 0) & (source < n_slab) & ((end & (direct == slab)) | (shared == slab) | (mate == slab))

    senders = {offset: sends_here(offset) for offset in OFFSETS}
    for offset in OFFSETS:
        @pl.when(greets(offset))
        def _():
            pl.semaphore_signal(barrier, inc=1, device_id=(slab + offset, grp), device_id_type=MESH)
    pl.semaphore_signal(barrier, inc=1, device_id=(slab, grp_mate), device_id_type=MESH)

    per = rows // CHUNKS
    p_copies = [
        pltpu.make_async_copy(
            p_hbm.at[pl.ds(i * per, per)], ext.at[pl.ds(rows + i * per, per)], p_sem.at[i]
        )
        for i in range(CHUNKS)
    ]
    for copy in p_copies:
        copy.start()
    m_copy = pltpu.make_async_copy(m_hbm, m_buf, in_sem.at[1])
    small = [
        pltpu.make_async_copy(agg_hbm, agg, in_sem.at[2]),
        pltpu.make_async_copy(pair_hbm, pair, in_sem.at[3]),
        pltpu.make_async_copy(nbr_hbm, nbr, in_sem.at[4]),
    ]
    for copy in small:
        copy.start()
    a_chunks = a_sem.shape[0]
    a_rows = rows // a_chunks
    a_copies = [
        pltpu.make_async_copy(a_hbm.at[pl.ds(i * a_rows, a_rows)], a_buf.at[pl.ds(i * a_rows, a_rows)], a_sem.at[i])
        for i in range(a_chunks)
    ]
    for copy in a_copies:
        copy.start()
    m_copy.start()

    def halo_copy(side, chunk):
        span = pl.ds(chunk * per, per)
        target = slab + 1 - 2 * side
        return pltpu.make_async_remote_copy(
            src_ref=p_fold.at[span],
            dst_ref=halo.at[side, span],
            send_sem=halo_send.at[side, chunk],
            recv_sem=halo_recv.at[side, chunk],
            device_id=(target, grp),
            device_id_type=MESH,
        )

    has_next = slab < n_slab - 1
    has_previous = slab > 0
    for chunk in range(CHUNKS):
        p_copies[chunk].wait()

        def fold_row(r, _, chunk=chunk):
            p_fold[chunk * per + r] = fold(ext[rows + chunk * per + r])
            return 0

        lax.fori_loop(0, per, fold_row, 0, unroll=per)
        if chunk == 0:
            pl.semaphore_wait(barrier, jnp.where((slab < 2) | (slab >= n_slab - 2), 4, 3))

        @pl.when(has_next)
        def _():
            halo_copy(0, chunk).start()

        @pl.when(has_previous)
        def _():
            halo_copy(1, chunk).start()

    tall = 64
    sub = lax.broadcasted_iota(jnp.int32, (tall, 128), 0)
    lane = lax.broadcasted_iota(jnp.int32, (tall, 128), 1)
    lane_row = lax.broadcasted_iota(jnp.int32, (1, 128), 1)
    tab_v[...] = jnp.zeros_like(tab_v)
    for copy in small:
        copy.wait()
    tab_v[0:1, 0:rows] = agg[...]
    ids = tab_v[0:1, :]
    owner_row = lax.div(ids, jnp.int32(n_grp * aggs))
    inside = lax.rem(ids, jnp.int32(aggs))
    at = jnp.zeros_like(owner_row)
    for q in range(WINDOW):
        at = at + jnp.where(owner_row == owner_of[q], q, 0)
    far = 1000
    key_row = jnp.where(lane_row < rows, at * aggs + inside, far).astype(F32)
    keys = jnp.broadcast_to(key_row, (tall, 128))
    key_col = jnp.sum(jnp.where(sub == lane, keys, 0.0), axis=1, keepdims=True)
    less = (keys < key_col) | ((keys == key_col) & (lane < sub))
    rank = jnp.sum(jnp.where(less, 1.0, 0.0), axis=1, keepdims=True)
    lane_f = lane.astype(F32)
    hit = rank == lane_f
    order_row = jnp.sum(jnp.where(hit, sub.astype(F32), 0.0), axis=0, keepdims=True)
    sorted_row = jnp.sum(jnp.where(hit, key_col, 0.0), axis=0, keepdims=True)
    same = (sorted_row == pltpu.roll(sorted_row, 1, 1)) & (lane_row > 0)
    before_row = jnp.where(same, lane_row - 1, rows)
    upto = jnp.sum(jnp.where(key_col <= lane_f, 1.0, 0.0), axis=0, keepdims=True)
    below = jnp.sum(jnp.where(key_col < lane_f, 1.0, 0.0), axis=0, keepdims=True)
    last_row = jnp.where(upto > below, upto - 1.0, float(rows))
    named_row = jnp.zeros((tall, 128), F32)
    named_col = jnp.zeros((tall, 128), F32)
    for i in range(half):
        named_row = named_row + jnp.where(lane == pair[0, i], 1.0, 0.0)
        named_col = named_col + jnp.where(sub == pair[0, i], 1.0, 0.0)
    free_row = (named_row == 0.0) & (lane < aggs)
    free_col = (named_col == 0.0) & (sub < aggs)
    rank_free = jnp.sum(jnp.where(free_row & (lane < sub), 1.0, 0.0), axis=1, keepdims=True)
    rest_row = jnp.sum(
        jnp.where(free_col & (rank_free == lane_f), sub.astype(F32), 0.0), axis=0, keepdims=True
    )
    tab_v[0:1, :] = order_row.astype(jnp.int32)
    tab_v[1:2, :] = before_row
    tab_v[2:3, :] = last_row.astype(jnp.int32)
    tab_v[3:4, :] = rest_row.astype(jnp.int32)
    tab_copy = pltpu.make_async_copy(tab_v, tab, tab_sem)
    tab_copy.start()

    run[rows] = jnp.zeros((width, width), F32)
    for i in range(a_chunks):
        a_copies[i].wait()

        def lay(r, _, i=i):
            row = i * a_rows + r
            a_cat[row] = jnp.concatenate([a_buf[row, n] for n in range(slots)], axis=1)
            p_t[row] = ext[rows + row].T
            return 0

        lax.fori_loop(0, a_rows, lay, 0, unroll=a_rows)
    m_copy.wait()

    def turn(k, _):
        m_t[k] = m_buf[k].T
        return 0

    lax.fori_loop(0, aggs, turn, 0, unroll=half)
    tab_copy.wait()

    for side, there in ((0, has_previous), (1, has_next)):
        base = side * 2 * rows

        @pl.when(jnp.logical_not(there))
        def _():
            def clear(r, _):
                ext[base + r] = jnp.zeros((width, width), BF16)
                return 0

            lax.fori_loop(0, rows, clear, 0, unroll=2)

    for chunk in range(CHUNKS):
        for side, there in ((0, has_previous), (1, has_next)):
            base = side * 2 * rows + chunk * per

            @pl.when(there)
            def _():
                halo_copy(side, chunk).wait_recv()

                def open_row(r, _):
                    ext[base + r] = unfold(halo[side, chunk * per + r])
                    return 0

                lax.fori_loop(0, per, open_row, 0, unroll=per)

    def part_copy(q, piece=0):
        owner = owner_of[q]
        at_owner = slab - owner + REACH
        if q == HANDED:
            source, target, arrived = hand, handed, hand_recv
        else:
            span = pl.ds(piece * half, half)
            source, target, arrived = send.at[q, span], recv.at[at_owner, span], part_recv.at[at_owner, piece]
        return pltpu.make_async_remote_copy(
            src_ref=source,
            dst_ref=target,
            send_sem=part_send.at[q, piece],
            recv_sem=arrived,
            device_id=(chip_mate if q == HANDED else owner, grp),
            device_id_type=MESH,
        )

    leaves = {
        0: ((0, 0), (0, 1)),
        HANDED: ((HANDED, 0),),
        SHARED: ((SHARED, 0), (SHARED, 1)),
        3: ((3, 0), (3, 1)),
    }

    def row_at(k):
        return jnp.clip(tab[0, k], 0, rows - 1)

    def weigh(k, _):
        r = row_at(k)
        picked = jnp.concatenate(
            [ext[jnp.clip(nbr[n, r], 0, 3 * rows - 1)] for n in range(slots)], axis=0
        )
        w_buf[k] = jnp.dot(a_cat[r], picked, preferred_element_type=F32).astype(BF16)
        return 0

    def project(k, _):
        part = jnp.dot(p_t[row_at(k)], w_buf[k], preferred_element_type=F32)
        run[k] = part + run[jnp.clip(tab[1, k], 0, rows)]
        return 0

    for q in range(WINDOW):
        begin, end = q * capacity, min((q + 1) * capacity, rows)
        lax.fori_loop(begin, end, weigh, 0, unroll=end - begin)
        lax.fori_loop(begin, end, project, 0, unroll=end - begin)

        def gather(k, _, q=q):
            block = fold(run[jnp.clip(tab[2, q * aggs + k], 0, rows)])
            if q == HANDED:
                hand[k] = block
            elif q == SHARED:
                send[q, k] = (block + handed[k]).astype(BF16)
            elif q < REACH:
                send[q, k] = block.astype(BF16)
            else:
                acc[k] = block
            return 0

        if q == SHARED:
            part_copy(HANDED).wait_recv()

        lax.fori_loop(0, aggs, gather, 0, unroll=aggs)
        for which in leaves.get(q, ()):
            part_copy(*which).start()

    for offset in OFFSETS:
        at_here = offset + REACH

        @pl.when(senders[offset])
        def _():
            for piece in range(2):
                span = pl.ds(piece * half, half)
                pltpu.make_async_remote_copy(
                    src_ref=recv.at[at_here, span],
                    dst_ref=recv.at[at_here, span],
                    send_sem=part_send.at[0, piece],
                    recv_sem=part_recv.at[at_here, piece],
                    device_id=(slab, grp),
                    device_id_type=MESH,
                ).wait_recv()
                acc[span] += recv[at_here, span].astype(F32)

    def open_sum(k, _):
        one_buf[k] = unfold(acc[k])
        return 0

    lax.fori_loop(0, aggs, open_sum, 0, unroll=aggs)

    def away(t, _):
        k = jnp.where(parity == 0, half + t, jnp.clip(tab[3, t], 0, aggs - 1))
        tx[t] = fold(galerkin(one_buf[k], m_t[k], m_buf[k])).astype(BF16)
        return 0

    cut = (half + 1) // 2
    pair_copies = []
    for piece, (begin, end) in enumerate(((0, cut), (cut, half))):
        lax.fori_loop(begin, end, away, 0, unroll=end - begin)
        span = pl.ds(begin, end - begin)
        pair_copies.append(
            pltpu.make_async_remote_copy(
                src_ref=tx.at[span], dst_ref=rx.at[span],
                send_sem=pair_send.at[piece], recv_sem=pair_recv.at[piece],
                device_id=(slab, grp_mate), device_id_type=MESH,
            )
        )
        pair_copies[-1].start()

    def home(t, _):
        k = jnp.where(parity == 0, t, jnp.clip(pair[0, t], 0, aggs - 1))
        two[t] = fold(galerkin(one_buf[k], m_t[k], m_buf[k]))
        return 0

    lax.fori_loop(0, half, home, 0, unroll=half)
    at_rx = []
    for t in range(half):
        before = sum((pair[0, i] < pair[0, t]).astype(jnp.int32) for i in range(half))
        at_rx.append(jnp.where(parity == 0, jnp.clip(before, 0, half - 1), t))
    for copy in pair_copies:
        copy.wait_recv()
    for t in range(half):
        two[t] += rx[at_rx[t]].astype(F32)

    for copy in pair_copies:
        copy.wait_send()
    for which in sum(leaves.values(), ()):
        part_copy(*which).wait_send()
    for chunk in range(CHUNKS):
        @pl.when(has_next)
        def _():
            halo_copy(0, chunk).wait_send()

        @pl.when(has_previous)
        def _():
            halo_copy(1, chunk).wait_send()


def spread(acc, two_folded, one_hbm, two_hbm, one_buf, two_buf, sem):
    for k in range(acc.shape[0]):
        one_buf[k] = unfold(acc[k])
    one_copy = pltpu.make_async_copy(one_buf, one_hbm, sem.at[0])
    one_copy.start()
    for k in range(two_folded.shape[0]):
        two_buf[k] = unfold(two_folded[k])
    two_copy = pltpu.make_async_copy(two_buf, two_hbm, sem.at[1])
    two_copy.start()
    one_copy.wait()
    two_copy.wait()


def on_device(n_slab, n_grp, a_blocks, neighbors, prolong, agg_ids, coarse_prolong, pairing):
    rows, slots, width, _ = a_blocks.shape
    aggs = coarse_prolong.shape[0]
    half = aggs // 2
    sizes = (n_slab, n_grp, rows, slots, width, aggs)
    a_chunks = 7
    dma = pltpu.SemaphoreType.DMA
    scratch = [
        pltpu.SMEM((slots, rows), jnp.int32),
        pltpu.VMEM((1, rows), jnp.int32),
        pltpu.SMEM((1, half), jnp.int32),
        pltpu.VMEM((rows, slots, width, width), BF16),
        pltpu.VMEM((rows, width, slots * width), BF16),
        pltpu.VMEM((3 * rows, width, width), BF16),
        pltpu.VMEM((rows, width // 2, 2 * width), BF16),
        pltpu.VMEM((2, rows, width // 2, 2 * width), BF16),
        pltpu.VMEM((rows, width, width), BF16),
        pltpu.VMEM((aggs, width, width), BF16),
        pltpu.VMEM((aggs, width, width), BF16),
        pltpu.VMEM((rows, width, width), BF16),
        pltpu.VMEM((rows + 1, width, width), F32),
        pltpu.VMEM((REACH, aggs, width // 2, 2 * width), BF16),
        pltpu.VMEM((2 * REACH + 1, aggs, width // 2, 2 * width), BF16),
        pltpu.VMEM((aggs, width // 2, 2 * width), F32),
        pltpu.VMEM((aggs, width // 2, 2 * width), F32),
        pltpu.VMEM((aggs, width, width), F32),
        pltpu.VMEM((half, width // 2, 2 * width), BF16),
        pltpu.VMEM((half, width // 2, 2 * width), BF16),
        pltpu.VMEM((8, 128), jnp.int32),
        pltpu.SMEM((8, 128), jnp.int32),
        dma((a_chunks,)),
        dma((CHUNKS,)),
        dma((5,)),
        dma,
        dma((2, CHUNKS)),
        dma((2, CHUNKS)),
        dma((REACH, 2)),
        dma((2 * REACH + 1, 2)),
        dma,
        dma((2,)),
        dma((2,)),
    ]
    vmem = pl.BlockSpec(memory_space=pltpu.VMEM)
    hbm = pl.BlockSpec(memory_space=pltpu.HBM)
    folded = pl.pallas_call(
        functools.partial(kernel, sizes),
        out_shape=(
            jax.ShapeDtypeStruct((aggs, width // 2, 2 * width), F32),
            jax.ShapeDtypeStruct((half, width // 2, 2 * width), F32),
        ),
        in_specs=[hbm] * 6,
        out_specs=(vmem, vmem),
        scratch_shapes=scratch,
        compiler_params=pltpu.CompilerParams(
            collective_id=0, has_side_effects=True, vmem_limit_bytes=30 * 2**20
        ),
    )(*(pltpu.with_memory_space_constraint(x, pltpu.HBM) for x in (neighbors.T, agg_ids.reshape(1, rows), pairing, a_blocks, prolong, coarse_prolong)))
    return pl.pallas_call(
        spread,
        out_shape=(
            jax.ShapeDtypeStruct((aggs, width, width), F32),
            jax.ShapeDtypeStruct((half, width, width), F32),
        ),
        in_specs=[vmem, vmem],
        out_specs=(hbm, hbm),
        scratch_shapes=[
            pltpu.VMEM((aggs, width, width), F32),
            pltpu.VMEM((half, width, width), F32),
            dma((2,)),
        ],
        compiler_params=pltpu.CompilerParams(vmem_limit_bytes=4 * 2**20),
    )(*folded)


def solution(mesh):
    placed = (
        P(("slab", "grp"), None, None, None),
        P(("slab", "grp"), None),
        P(("slab", "grp"), None, None),
        P(("slab", "grp")),
        P(("slab", "grp"), None, None),
        P(("slab", "grp"), None),
    )
    return jax.shard_map(
        functools.partial(on_device, mesh.shape["slab"], mesh.shape["grp"]),
        mesh=mesh,
        in_specs=placed,
        out_specs=(P(("slab", "grp"), None, None), P(("slab", "grp"), None, None)),
        check_vma=False,
    )
```

```python
import functools

import jax
import jax.numpy as jnp
from jax import lax
from jax.experimental import pallas as pl
from jax.experimental.pallas import tpu as pltpu
from jax.sharding import PartitionSpec as P

MESH = pl.DeviceIdType.MESH
WINDOW = 5
REACH = WINDOW - 1
HANDED, SHARED = 1, 2
OFFSETS = (4, 2, 1, -1, -2, -4)
CHUNKS = 8
F32 = jnp.float32
BF16 = jnp.bfloat16


def fold(block):
    half = block.shape[0] // 2
    return jnp.concatenate([block[:half], block[half:]], axis=1)


def unfold(block):
    width = block.shape[1] // 2
    return jnp.concatenate([block[:, :width], block[:, width:]], axis=0)


def galerkin(block, map_t, map_):
    high = block.astype(BF16)
    low = (block - high.astype(F32)).astype(BF16)
    inner = jnp.dot(map_t, high, preferred_element_type=F32) + jnp.dot(
        map_t, low, preferred_element_type=F32
    )
    high = inner.astype(BF16)
    low = (inner - high.astype(F32)).astype(BF16)
    return jnp.dot(high, map_, preferred_element_type=F32) + jnp.dot(
        low, map_, preferred_element_type=F32
    )


def kernel(
    sizes,
    nbr_hbm, agg_hbm, pair_hbm, a_hbm, p_hbm, m_hbm,
    acc, two,
    nbr, agg, pair, a_buf, a_cat, ext, p_fold, halo, p_t, m_buf, m_t, w_buf, run, send, recv, hand, handed, one_buf, tx, rx, tab_v, tab,
    a_sem, p_sem, in_sem, tab_sem, halo_send, halo_recv, part_send, part_recv, hand_recv, pair_send, pair_recv,
):
    n_slab, n_grp, rows, slots, width, aggs = sizes
    half = aggs // 2
    capacity = (rows + WINDOW - 1) // WINDOW
    slab = lax.axis_index("slab")
    grp = lax.axis_index("grp")

    def owners(s):
        odd = s % 2
        side = 1 - 2 * odd
        low, high = s < 2, s >= n_slab - 2
        end = low | high
        direct = jnp.where(low, 2, jnp.where(high, n_slab - 3, s - 2 * side))
        far = jnp.where(low, 4, n_slab - 5)
        near = jnp.where(low, 3, n_slab - 4)
        outer = jnp.where(low, odd == 0, odd == 1)
        handed = jnp.where(end, jnp.where(outer, near, far), s + 2 * side)
        shared = jnp.where(end, jnp.where(outer, far, near), s - side)
        return direct, handed, shared, s + side, s

    owner_of = owners(slab)
    chip_mate = owner_of[3]
    grp_mate = grp + 1 - 2 * (grp % 2)
    parity = grp % 2

    barrier = pltpu.get_barrier_semaphore()

    def sends_here(offset):
        source = slab + offset
        direct, _, shared, mate, _ = owners(source)
        return (source >= 0) & (source < n_slab) & ((direct == slab) | (shared == slab) | (mate == slab))

    def greets(offset):
        source = slab + offset
        direct, _, shared, mate, _ = owners(source)
        end = (source < 2) | (source >= n_slab - 2)
        return (source >= 0) & (source < n_slab) & ((end & (direct == slab)) | (shared == slab) | (mate == slab))

    senders = {offset: sends_here(offset) for offset in OFFSETS}
    for offset in OFFSETS:
        @pl.when(greets(offset))
        def _():
            pl.semaphore_signal(barrier, inc=1, device_id=(slab + offset, grp), device_id_type=MESH)
    pl.semaphore_signal(barrier, inc=1, device_id=(slab, grp_mate), device_id_type=MESH)

    per = rows // CHUNKS
    p_copies = [
        pltpu.make_async_copy(
            p_hbm.at[pl.ds(i * per, per)], ext.at[pl.ds(rows + i * per, per)], p_sem.at[i]
        )
        for i in range(CHUNKS)
    ]
    for copy in p_copies:
        copy.start()
    m_copy = pltpu.make_async_copy(m_hbm, m_buf, in_sem.at[1])
    small = [
        pltpu.make_async_copy(agg_hbm, agg, in_sem.at[2]),
        pltpu.make_async_copy(pair_hbm, pair, in_sem.at[3]),
        pltpu.make_async_copy(nbr_hbm, nbr, in_sem.at[4]),
    ]
    for copy in small:
        copy.start()
    a_chunks = a_sem.shape[0]
    a_rows = rows // a_chunks
    a_copies = [
        pltpu.make_async_copy(a_hbm.at[pl.ds(i * a_rows, a_rows)], a_buf.at[pl.ds(i * a_rows, a_rows)], a_sem.at[i])
        for i in range(a_chunks)
    ]
    for copy in a_copies:
        copy.start()
    m_copy.start()

    def halo_copy(side, chunk):
        span = pl.ds(chunk * per, per)
        target = slab + 1 - 2 * side
        return pltpu.make_async_remote_copy(
            src_ref=p_fold.at[span],
            dst_ref=halo.at[side, span],
            send_sem=halo_send.at[side, chunk],
            recv_sem=halo_recv.at[side, chunk],
            device_id=(target, grp),
            device_id_type=MESH,
        )

    has_next = slab < n_slab - 1
    has_previous = slab > 0
    for chunk in range(CHUNKS):
        p_copies[chunk].wait()

        def fold_row(r, _, chunk=chunk):
            p_fold[chunk * per + r] = fold(ext[rows + chunk * per + r])
            return 0

        lax.fori_loop(0, per, fold_row, 0, unroll=per)
        if chunk == 0:
            pl.semaphore_wait(barrier, jnp.where((slab < 2) | (slab >= n_slab - 2), 4, 3))

        @pl.when(has_next)
        def _():
            halo_copy(0, chunk).start()

        @pl.when(has_previous)
        def _():
            halo_copy(1, chunk).start()

    tall = 64
    sub = lax.broadcasted_iota(jnp.int32, (tall, 128), 0)
    lane = lax.broadcasted_iota(jnp.int32, (tall, 128), 1)
    lane_row = lax.broadcasted_iota(jnp.int32, (1, 128), 1)
    tab_v[...] = jnp.zeros_like(tab_v)
    for copy in small:
        copy.wait()
    tab_v[0:1, 0:rows] = agg[...]
    ids = tab_v[0:1, :]
    owner_row = lax.div(ids, jnp.int32(n_grp * aggs))
    inside = lax.rem(ids, jnp.int32(aggs))
    at = jnp.zeros_like(owner_row)
    for q in range(WINDOW):
        at = at + jnp.where(owner_row == owner_of[q], q, 0)
    far = 1000
    key_row = jnp.where(lane_row < rows, at * aggs + inside, far).astype(F32)
    keys = jnp.broadcast_to(key_row, (tall, 128))
    key_col = jnp.sum(jnp.where(sub == lane, keys, 0.0), axis=1, keepdims=True)
    less = (keys < key_col) | ((keys == key_col) & (lane < sub))
    rank = jnp.sum(jnp.where(less, 1.0, 0.0), axis=1, keepdims=True)
    lane_f = lane.astype(F32)
    hit = rank == lane_f
    order_row = jnp.sum(jnp.where(hit, sub.astype(F32), 0.0), axis=0, keepdims=True)
    sorted_row = jnp.sum(jnp.where(hit, key_col, 0.0), axis=0, keepdims=True)
    same = (sorted_row == pltpu.roll(sorted_row, 1, 1)) & (lane_row > 0)
    before_row = jnp.where(same, lane_row - 1, rows)
    upto = jnp.sum(jnp.where(key_col <= lane_f, 1.0, 0.0), axis=0, keepdims=True)
    below = jnp.sum(jnp.where(key_col < lane_f, 1.0, 0.0), axis=0, keepdims=True)
    last_row = jnp.where(upto > below, upto - 1.0, float(rows))
    named_row = jnp.zeros((tall, 128), F32)
    named_col = jnp.zeros((tall, 128), F32)
    for i in range(half):
        named_row = named_row + jnp.where(lane == pair[0, i], 1.0, 0.0)
        named_col = named_col + jnp.where(sub == pair[0, i], 1.0, 0.0)
    free_row = (named_row == 0.0) & (lane < aggs)
    free_col = (named_col == 0.0) & (sub < aggs)
    rank_free = jnp.sum(jnp.where(free_row & (lane < sub), 1.0, 0.0), axis=1, keepdims=True)
    rest_row = jnp.sum(
        jnp.where(free_col & (rank_free == lane_f), sub.astype(F32), 0.0), axis=0, keepdims=True
    )
    tab_v[0:1, :] = order_row.astype(jnp.int32)
    tab_v[1:2, :] = before_row
    tab_v[2:3, :] = last_row.astype(jnp.int32)
    tab_v[3:4, :] = rest_row.astype(jnp.int32)
    tab_copy = pltpu.make_async_copy(tab_v, tab, tab_sem)
    tab_copy.start()

    run[rows] = jnp.zeros((width, width), F32)
    for i in range(a_chunks):
        a_copies[i].wait()

        def lay(r, _, i=i):
            row = i * a_rows + r
            a_cat[row] = jnp.concatenate([a_buf[row, n] for n in range(slots)], axis=1)
            p_t[row] = ext[rows + row].T
            return 0

        lax.fori_loop(0, a_rows, lay, 0, unroll=a_rows)
    m_copy.wait()

    def turn(k, _):
        m_t[k] = m_buf[k].T
        return 0

    lax.fori_loop(0, aggs, turn, 0, unroll=half)
    tab_copy.wait()

    for side, there in ((0, has_previous), (1, has_next)):
        base = side * 2 * rows

        @pl.when(jnp.logical_not(there))
        def _():
            def clear(r, _):
                ext[base + r] = jnp.zeros((width, width), BF16)
                return 0

            lax.fori_loop(0, rows, clear, 0, unroll=2)

    for chunk in range(CHUNKS):
        for side, there in ((0, has_previous), (1, has_next)):
            base = side * 2 * rows + chunk * per

            @pl.when(there)
            def _():
                halo_copy(side, chunk).wait_recv()

                def open_row(r, _):
                    ext[base + r] = unfold(halo[side, chunk * per + r])
                    return 0

                lax.fori_loop(0, per, open_row, 0, unroll=per)

    def part_copy(q, piece=0):
        owner = owner_of[q]
        at_owner = slab - owner + REACH
        if q == HANDED:
            source, target, arrived = hand, handed, hand_recv
        else:
            span = pl.ds(piece * half, half)
            source, target, arrived = send.at[q, span], recv.at[at_owner, span], part_recv.at[at_owner, piece]
        return pltpu.make_async_remote_copy(
            src_ref=source,
            dst_ref=target,
            send_sem=part_send.at[q, piece],
            recv_sem=arrived,
            device_id=(chip_mate if q == HANDED else owner, grp),
            device_id_type=MESH,
        )

    leaves = {
        0: ((0, 0), (0, 1)),
        HANDED: ((HANDED, 0),),
        SHARED: ((SHARED, 0), (SHARED, 1)),
        3: ((3, 0), (3, 1)),
    }

    def row_at(k):
        return jnp.clip(tab[0, k], 0, rows - 1)

    def weigh(k, _):
        r = row_at(k)
        picked = jnp.concatenate(
            [ext[nbr[n, r]] for n in range(slots)], axis=0
        )
        w_buf[k] = jnp.dot(a_cat[r], picked, preferred_element_type=F32).astype(BF16)
        return 0

    def project(k, _):
        part = jnp.dot(p_t[row_at(k)], w_buf[k], preferred_element_type=F32)
        run[k] = part + run[jnp.clip(tab[1, k], 0, rows)]
        return 0

    for q in range(WINDOW):
        begin, end = q * capacity, min((q + 1) * capacity, rows)
        lax.fori_loop(begin, end, weigh, 0, unroll=end - begin)
        lax.fori_loop(begin, end, project, 0, unroll=end - begin)

        def gather(k, _, q=q):
            block = fold(run[jnp.clip(tab[2, q * aggs + k], 0, rows)])
            if q == HANDED:
                hand[k] = block
            elif q == SHARED:
                send[q, k] = (block + handed[k]).astype(BF16)
            elif q < REACH:
                send[q, k] = block.astype(BF16)
            else:
                acc[k] = block
            return 0

        if q == SHARED:
            part_copy(HANDED).wait_recv()

        lax.fori_loop(0, aggs, gather, 0, unroll=aggs)
        for which in leaves.get(q, ()):
            part_copy(*which).start()

    for offset in OFFSETS:
        at_here = offset + REACH

        @pl.when(senders[offset])
        def _():
            for piece in range(2):
                span = pl.ds(piece * half, half)
                pltpu.make_async_remote_copy(
                    src_ref=recv.at[at_here, span],
                    dst_ref=recv.at[at_here, span],
                    send_sem=part_send.at[0, piece],
                    recv_sem=part_recv.at[at_here, piece],
                    device_id=(slab, grp),
                    device_id_type=MESH,
                ).wait_recv()
                acc[span] += recv[at_here, span].astype(F32)

    def open_sum(k, _):
        one_buf[k] = unfold(acc[k])
        return 0

    lax.fori_loop(0, aggs, open_sum, 0, unroll=aggs)

    def away(t, _):
        k = jnp.where(parity == 0, half + t, jnp.clip(tab[3, t], 0, aggs - 1))
        tx[t] = fold(galerkin(one_buf[k], m_t[k], m_buf[k])).astype(BF16)
        return 0

    cut = (half + 1) // 2
    pair_copies = []
    for piece, (begin, end) in enumerate(((0, cut), (cut, half))):
        lax.fori_loop(begin, end, away, 0, unroll=end - begin)
        span = pl.ds(begin, end - begin)
        pair_copies.append(
            pltpu.make_async_remote_copy(
                src_ref=tx.at[span], dst_ref=rx.at[span],
                send_sem=pair_send.at[piece], recv_sem=pair_recv.at[piece],
                device_id=(slab, grp_mate), device_id_type=MESH,
            )
        )
        pair_copies[-1].start()

    def home(t, _):
        k = jnp.where(parity == 0, t, jnp.clip(pair[0, t], 0, aggs - 1))
        two[t] = fold(galerkin(one_buf[k], m_t[k], m_buf[k]))
        return 0

    lax.fori_loop(0, half, home, 0, unroll=half)
    at_rx = []
    for t in range(half):
        before = sum((pair[0, i] < pair[0, t]).astype(jnp.int32) for i in range(half))
        at_rx.append(jnp.where(parity == 0, jnp.clip(before, 0, half - 1), t))
    for copy in pair_copies:
        copy.wait_recv()
    for t in range(half):
        two[t] += rx[at_rx[t]].astype(F32)

    for copy in pair_copies:
        copy.wait_send()
    for which in sum(leaves.values(), ()):
        part_copy(*which).wait_send()
    for chunk in range(CHUNKS):
        @pl.when(has_next)
        def _():
            halo_copy(0, chunk).wait_send()

        @pl.when(has_previous)
        def _():
            halo_copy(1, chunk).wait_send()


def spread(acc, two_folded, one_hbm, two_hbm, one_buf, two_buf, sem):
    for k in range(acc.shape[0]):
        one_buf[k] = unfold(acc[k])
    one_copy = pltpu.make_async_copy(one_buf, one_hbm, sem.at[0])
    one_copy.start()
    for k in range(two_folded.shape[0]):
        two_buf[k] = unfold(two_folded[k])
    two_copy = pltpu.make_async_copy(two_buf, two_hbm, sem.at[1])
    two_copy.start()
    one_copy.wait()
    two_copy.wait()


def on_device(n_slab, n_grp, a_blocks, neighbors, prolong, agg_ids, coarse_prolong, pairing):
    rows, slots, width, _ = a_blocks.shape
    aggs = coarse_prolong.shape[0]
    half = aggs // 2
    sizes = (n_slab, n_grp, rows, slots, width, aggs)
    a_chunks = 7
    dma = pltpu.SemaphoreType.DMA
    scratch = [
        pltpu.SMEM((slots, rows), jnp.int32),
        pltpu.VMEM((1, rows), jnp.int32),
        pltpu.SMEM((1, half), jnp.int32),
        pltpu.VMEM((rows, slots, width, width), BF16),
        pltpu.VMEM((rows, width, slots * width), BF16),
        pltpu.VMEM((3 * rows, width, width), BF16),
        pltpu.VMEM((rows, width // 2, 2 * width), BF16),
        pltpu.VMEM((2, rows, width // 2, 2 * width), BF16),
        pltpu.VMEM((rows, width, width), BF16),
        pltpu.VMEM((aggs, width, width), BF16),
        pltpu.VMEM((aggs, width, width), BF16),
        pltpu.VMEM((rows, width, width), BF16),
        pltpu.VMEM((rows + 1, width, width), F32),
        pltpu.VMEM((REACH, aggs, width // 2, 2 * width), BF16),
        pltpu.VMEM((2 * REACH + 1, aggs, width // 2, 2 * width), BF16),
        pltpu.VMEM((aggs, width // 2, 2 * width), F32),
        pltpu.VMEM((aggs, width // 2, 2 * width), F32),
        pltpu.VMEM((aggs, width, width), F32),
        pltpu.VMEM((half, width // 2, 2 * width), BF16),
        pltpu.VMEM((half, width // 2, 2 * width), BF16),
        pltpu.VMEM((8, 128), jnp.int32),
        pltpu.SMEM((8, 128), jnp.int32),
        dma((a_chunks,)),
        dma((CHUNKS,)),
        dma((5,)),
        dma,
        dma((2, CHUNKS)),
        dma((2, CHUNKS)),
        dma((REACH, 2)),
        dma((2 * REACH + 1, 2)),
        dma,
        dma((2,)),
        dma((2,)),
    ]
    vmem = pl.BlockSpec(memory_space=pltpu.VMEM)
    hbm = pl.BlockSpec(memory_space=pltpu.HBM)
    folded = pl.pallas_call(
        functools.partial(kernel, sizes),
        out_shape=(
            jax.ShapeDtypeStruct((aggs, width // 2, 2 * width), F32),
            jax.ShapeDtypeStruct((half, width // 2, 2 * width), F32),
        ),
        in_specs=[hbm] * 6,
        out_specs=(vmem, vmem),
        scratch_shapes=scratch,
        compiler_params=pltpu.CompilerParams(
            collective_id=0, has_side_effects=True, vmem_limit_bytes=30 * 2**20
        ),
    )(*(pltpu.with_memory_space_constraint(x, pltpu.HBM) for x in (neighbors.T, agg_ids.reshape(1, rows), pairing, a_blocks, prolong, coarse_prolong)))
    return pl.pallas_call(
        spread,
        out_shape=(
            jax.ShapeDtypeStruct((aggs, width, width), F32),
            jax.ShapeDtypeStruct((half, width, width), F32),
        ),
        in_specs=[vmem, vmem],
        out_specs=(hbm, hbm),
        scratch_shapes=[
            pltpu.VMEM((aggs, width, width), F32),
            pltpu.VMEM((half, width, width), F32),
            dma((2,)),
        ],
        compiler_params=pltpu.CompilerParams(vmem_limit_bytes=4 * 2**20),
    )(*folded)


def solution(mesh):
    placed = (
        P(("slab", "grp"), None, None, None),
        P(("slab", "grp"), None),
        P(("slab", "grp"), None, None),
        P(("slab", "grp")),
        P(("slab", "grp"), None, None),
        P(("slab", "grp"), None),
    )
    return jax.shard_map(
        functools.partial(on_device, mesh.shape["slab"], mesh.shape["grp"]),
        mesh=mesh,
        in_specs=placed,
        out_specs=(P(("slab", "grp"), None, None), P(("slab", "grp"), None, None)),
        check_vma=False,
    )
```

```python
import functools

import jax
import jax.numpy as jnp
from jax import lax
from jax.experimental import pallas as pl
from jax.experimental.pallas import tpu as pltpu
from jax.sharding import PartitionSpec as P

MESH = pl.DeviceIdType.MESH
WINDOW = 5
REACH = WINDOW - 1
HANDED, SHARED = 1, 2
OFFSETS = (4, 2, 1, -1, -2, -4)
CHUNKS = 8
F32 = jnp.float32
BF16 = jnp.bfloat16


def fold(block):
    half = block.shape[0] // 2
    return jnp.concatenate([block[:half], block[half:]], axis=1)


def unfold(block):
    width = block.shape[1] // 2
    return jnp.concatenate([block[:, :width], block[:, width:]], axis=0)


def galerkin(block, map_t, map_):
    high = block.astype(BF16)
    low = (block - high.astype(F32)).astype(BF16)
    inner = jnp.dot(map_t, high, preferred_element_type=F32) + jnp.dot(
        map_t, low, preferred_element_type=F32
    )
    high = inner.astype(BF16)
    low = (inner - high.astype(F32)).astype(BF16)
    return jnp.dot(high, map_, preferred_element_type=F32) + jnp.dot(
        low, map_, preferred_element_type=F32
    )


def kernel(
    sizes,
    nbr_hbm, agg_hbm, pair_hbm, a_hbm, p_hbm, m_hbm,
    acc, two,
    nbr, agg, pair, a_buf, a_cat, ext, p_fold, halo, p_t, m_buf, m_t, run, send, recv, hand, handed, one_buf, tx, rx, tab_v, tab,
    a_sem, p_sem, in_sem, tab_sem, halo_send, halo_recv, part_send, part_recv, hand_recv, pair_send, pair_recv,
):
    n_slab, n_grp, rows, slots, width, aggs = sizes
    half = aggs // 2
    capacity = (rows + WINDOW - 1) // WINDOW
    slab = lax.axis_index("slab")
    grp = lax.axis_index("grp")

    def owners(s):
        odd = s % 2
        side = 1 - 2 * odd
        low, high = s < 2, s >= n_slab - 2
        end = low | high
        direct = jnp.where(low, 2, jnp.where(high, n_slab - 3, s - 2 * side))
        far = jnp.where(low, 4, n_slab - 5)
        near = jnp.where(low, 3, n_slab - 4)
        outer = jnp.where(low, odd == 0, odd == 1)
        handed = jnp.where(end, jnp.where(outer, near, far), s + 2 * side)
        shared = jnp.where(end, jnp.where(outer, far, near), s - side)
        return direct, handed, shared, s + side, s

    owner_of = owners(slab)
    chip_mate = owner_of[3]
    grp_mate = grp + 1 - 2 * (grp % 2)
    parity = grp % 2

    barrier = pltpu.get_barrier_semaphore()

    def sends_here(offset):
        source = slab + offset
        direct, _, shared, mate, _ = owners(source)
        return (source >= 0) & (source < n_slab) & ((direct == slab) | (shared == slab) | (mate == slab))

    def greets(offset):
        source = slab + offset
        direct, _, shared, mate, _ = owners(source)
        end = (source < 2) | (source >= n_slab - 2)
        return (source >= 0) & (source < n_slab) & ((end & (direct == slab)) | (shared == slab) | (mate == slab))

    senders = {offset: sends_here(offset) for offset in OFFSETS}
    for offset in OFFSETS:
        @pl.when(greets(offset))
        def _():
            pl.semaphore_signal(barrier, inc=1, device_id=(slab + offset, grp), device_id_type=MESH)
    pl.semaphore_signal(barrier, inc=1, device_id=(slab, grp_mate), device_id_type=MESH)

    per = rows // CHUNKS
    p_copies = [
        pltpu.make_async_copy(
            p_hbm.at[pl.ds(i * per, per)], ext.at[pl.ds(rows + i * per, per)], p_sem.at[i]
        )
        for i in range(CHUNKS)
    ]
    for copy in p_copies:
        copy.start()
    m_copy = pltpu.make_async_copy(m_hbm, m_buf, in_sem.at[1])
    small = [
        pltpu.make_async_copy(agg_hbm, agg, in_sem.at[2]),
        pltpu.make_async_copy(pair_hbm, pair, in_sem.at[3]),
        pltpu.make_async_copy(nbr_hbm, nbr, in_sem.at[4]),
    ]
    for copy in small:
        copy.start()
    a_chunks = a_sem.shape[0]
    a_rows = rows // a_chunks
    a_copies = [
        pltpu.make_async_copy(a_hbm.at[pl.ds(i * a_rows, a_rows)], a_buf.at[pl.ds(i * a_rows, a_rows)], a_sem.at[i])
        for i in range(a_chunks)
    ]
    for copy in a_copies:
        copy.start()
    m_copy.start()

    def halo_copy(side, chunk):
        span = pl.ds(chunk * per, per)
        target = slab + 1 - 2 * side
        return pltpu.make_async_remote_copy(
            src_ref=p_fold.at[span],
            dst_ref=halo.at[side, span],
            send_sem=halo_send.at[side, chunk],
            recv_sem=halo_recv.at[side, chunk],
            device_id=(target, grp),
            device_id_type=MESH,
        )

    has_next = slab < n_slab - 1
    has_previous = slab > 0
    for chunk in range(CHUNKS):
        p_copies[chunk].wait()

        def fold_row(r, _, chunk=chunk):
            p_fold[chunk * per + r] = fold(ext[rows + chunk * per + r])
            return 0

        lax.fori_loop(0, per, fold_row, 0, unroll=per)
        if chunk == 0:
            pl.semaphore_wait(barrier, jnp.where((slab < 2) | (slab >= n_slab - 2), 4, 3))

        @pl.when(has_next)
        def _():
            halo_copy(0, chunk).start()

        @pl.when(has_previous)
        def _():
            halo_copy(1, chunk).start()

    tall = 64
    sub = lax.broadcasted_iota(jnp.int32, (tall, 128), 0)
    lane = lax.broadcasted_iota(jnp.int32, (tall, 128), 1)
    lane_row = lax.broadcasted_iota(jnp.int32, (1, 128), 1)
    tab_v[...] = jnp.zeros_like(tab_v)
    for copy in small:
        copy.wait()
    tab_v[0:1, 0:rows] = agg[...]
    ids = tab_v[0:1, :]
    owner_row = lax.div(ids, jnp.int32(n_grp * aggs))
    inside = lax.rem(ids, jnp.int32(aggs))
    at = jnp.zeros_like(owner_row)
    for q in range(WINDOW):
        at = at + jnp.where(owner_row == owner_of[q], q, 0)
    far = 1000
    key_row = jnp.where(lane_row < rows, at * aggs + inside, far).astype(F32)
    keys = jnp.broadcast_to(key_row, (tall, 128))
    key_col = jnp.sum(jnp.where(sub == lane, keys, 0.0), axis=1, keepdims=True)
    less = (keys < key_col) | ((keys == key_col) & (lane < sub))
    rank = jnp.sum(jnp.where(less, 1.0, 0.0), axis=1, keepdims=True)
    lane_f = lane.astype(F32)
    hit = rank == lane_f
    order_row = jnp.sum(jnp.where(hit, sub.astype(F32), 0.0), axis=0, keepdims=True)
    sorted_row = jnp.sum(jnp.where(hit, key_col, 0.0), axis=0, keepdims=True)
    same = (sorted_row == pltpu.roll(sorted_row, 1, 1)) & (lane_row > 0)
    before_row = jnp.where(same, lane_row - 1, rows)
    upto = jnp.sum(jnp.where(key_col <= lane_f, 1.0, 0.0), axis=0, keepdims=True)
    below = jnp.sum(jnp.where(key_col < lane_f, 1.0, 0.0), axis=0, keepdims=True)
    last_row = jnp.where(upto > below, upto - 1.0, float(rows))
    named_row = jnp.zeros((tall, 128), F32)
    named_col = jnp.zeros((tall, 128), F32)
    for i in range(half):
        named_row = named_row + jnp.where(lane == pair[0, i], 1.0, 0.0)
        named_col = named_col + jnp.where(sub == pair[0, i], 1.0, 0.0)
    free_row = (named_row == 0.0) & (lane < aggs)
    free_col = (named_col == 0.0) & (sub < aggs)
    rank_free = jnp.sum(jnp.where(free_row & (lane < sub), 1.0, 0.0), axis=1, keepdims=True)
    rest_row = jnp.sum(
        jnp.where(free_col & (rank_free == lane_f), sub.astype(F32), 0.0), axis=0, keepdims=True
    )
    tab_v[0:1, :] = order_row.astype(jnp.int32)
    tab_v[1:2, :] = before_row
    tab_v[2:3, :] = last_row.astype(jnp.int32)
    tab_v[3:4, :] = rest_row.astype(jnp.int32)
    tab_copy = pltpu.make_async_copy(tab_v, tab, tab_sem)
    tab_copy.start()

    run[rows] = jnp.zeros((width, width), F32)
    for i in range(a_chunks):
        a_copies[i].wait()

        def lay(r, _, i=i):
            row = i * a_rows + r
            a_cat[row] = jnp.concatenate([a_buf[row, n] for n in range(slots)], axis=1)
            p_t[row] = ext[rows + row].T
            return 0

        lax.fori_loop(0, a_rows, lay, 0, unroll=a_rows)
    m_copy.wait()

    def turn(k, _):
        m_t[k] = m_buf[k].T
        return 0

    lax.fori_loop(0, aggs, turn, 0, unroll=half)
    tab_copy.wait()

    for side, there in ((0, has_previous), (1, has_next)):
        base = side * 2 * rows

        @pl.when(jnp.logical_not(there))
        def _():
            def clear(r, _):
                ext[base + r] = jnp.zeros((width, width), BF16)
                return 0

            lax.fori_loop(0, rows, clear, 0, unroll=2)

    for chunk in range(CHUNKS):
        for side, there in ((0, has_previous), (1, has_next)):
            base = side * 2 * rows + chunk * per

            @pl.when(there)
            def _():
                halo_copy(side, chunk).wait_recv()

                def open_row(r, _):
                    ext[base + r] = unfold(halo[side, chunk * per + r])
                    return 0

                lax.fori_loop(0, per, open_row, 0, unroll=per)

    def part_copy(q, piece=0):
        owner = owner_of[q]
        at_owner = slab - owner + REACH
        if q == HANDED:
            source, target, arrived = hand, handed, hand_recv
        else:
            span = pl.ds(piece * half, half)
            source, target, arrived = send.at[q, span], recv.at[at_owner, span], part_recv.at[at_owner, piece]
        return pltpu.make_async_remote_copy(
            src_ref=source,
            dst_ref=target,
            send_sem=part_send.at[q, piece],
            recv_sem=arrived,
            device_id=(chip_mate if q == HANDED else owner, grp),
            device_id_type=MESH,
        )

    leaves = {
        0: ((0, 0), (0, 1)),
        HANDED: ((HANDED, 0),),
        SHARED: ((SHARED, 0), (SHARED, 1)),
        3: ((3, 0), (3, 1)),
    }

    def row_at(k):
        return jnp.clip(tab[0, k], 0, rows - 1)

    def weigh(k):
        r = row_at(k)
        picked = jnp.concatenate(
            [ext[nbr[n, r]] for n in range(slots)], axis=0
        )
        return jnp.dot(a_cat[r], picked, preferred_element_type=F32).astype(BF16)

    for q in range(WINDOW):
        begin, end = q * capacity, min((q + 1) * capacity, rows)
        weighed = [weigh(k) for k in range(begin, end)]
        parts = [
            jnp.dot(p_t[row_at(begin + i)], block, preferred_element_type=F32)
            for i, block in enumerate(weighed)
        ]
        for i, part in enumerate(parts):
            run[begin + i] = part + run[jnp.clip(tab[1, begin + i], 0, rows)]

        def gather(k, _, q=q):
            block = fold(run[jnp.clip(tab[2, q * aggs + k], 0, rows)])
            if q == HANDED:
                hand[k] = block
            elif q == SHARED:
                send[q, k] = (block + handed[k]).astype(BF16)
            elif q < REACH:
                send[q, k] = block.astype(BF16)
            else:
                acc[k] = block
            return 0

        if q == SHARED:
            part_copy(HANDED).wait_recv()

        lax.fori_loop(0, aggs, gather, 0, unroll=aggs)
        for which in leaves.get(q, ()):
            part_copy(*which).start()

    for offset in OFFSETS:
        at_here = offset + REACH

        @pl.when(senders[offset])
        def _():
            for piece in range(2):
                span = pl.ds(piece * half, half)
                pltpu.make_async_remote_copy(
                    src_ref=recv.at[at_here, span],
                    dst_ref=recv.at[at_here, span],
                    send_sem=part_send.at[0, piece],
                    recv_sem=part_recv.at[at_here, piece],
                    device_id=(slab, grp),
                    device_id_type=MESH,
                ).wait_recv()
                acc[span] += recv[at_here, span].astype(F32)

    def open_sum(k, _):
        one_buf[k] = unfold(acc[k])
        return 0

    lax.fori_loop(0, aggs, open_sum, 0, unroll=aggs)

    def away(t, _):
        k = jnp.where(parity == 0, half + t, jnp.clip(tab[3, t], 0, aggs - 1))
        tx[t] = fold(galerkin(one_buf[k], m_t[k], m_buf[k])).astype(BF16)
        return 0

    cut = (half + 1) // 2
    pair_copies = []
    for piece, (begin, end) in enumerate(((0, cut), (cut, half))):
        lax.fori_loop(begin, end, away, 0, unroll=end - begin)
        span = pl.ds(begin, end - begin)
        pair_copies.append(
            pltpu.make_async_remote_copy(
                src_ref=tx.at[span], dst_ref=rx.at[span],
                send_sem=pair_send.at[piece], recv_sem=pair_recv.at[piece],
                device_id=(slab, grp_mate), device_id_type=MESH,
            )
        )
        pair_copies[-1].start()

    def home(t, _):
        k = jnp.where(parity == 0, t, jnp.clip(pair[0, t], 0, aggs - 1))
        two[t] = fold(galerkin(one_buf[k], m_t[k], m_buf[k]))
        return 0

    lax.fori_loop(0, half, home, 0, unroll=half)
    at_rx = []
    for t in range(half):
        before = sum((pair[0, i] < pair[0, t]).astype(jnp.int32) for i in range(half))
        at_rx.append(jnp.where(parity == 0, jnp.clip(before, 0, half - 1), t))
    for copy in pair_copies:
        copy.wait_recv()
    for t in range(half):
        two[t] += rx[at_rx[t]].astype(F32)

    for copy in pair_copies:
        copy.wait_send()
    for which in sum(leaves.values(), ()):
        part_copy(*which).wait_send()
    for chunk in range(CHUNKS):
        @pl.when(has_next)
        def _():
            halo_copy(0, chunk).wait_send()

        @pl.when(has_previous)
        def _():
            halo_copy(1, chunk).wait_send()


def spread(acc, two_folded, one_hbm, two_hbm, one_buf, two_buf, sem):
    for k in range(acc.shape[0]):
        one_buf[k] = unfold(acc[k])
    one_copy = pltpu.make_async_copy(one_buf, one_hbm, sem.at[0])
    one_copy.start()
    for k in range(two_folded.shape[0]):
        two_buf[k] = unfold(two_folded[k])
    two_copy = pltpu.make_async_copy(two_buf, two_hbm, sem.at[1])
    two_copy.start()
    one_copy.wait()
    two_copy.wait()


def on_device(n_slab, n_grp, a_blocks, neighbors, prolong, agg_ids, coarse_prolong, pairing):
    rows, slots, width, _ = a_blocks.shape
    aggs = coarse_prolong.shape[0]
    half = aggs // 2
    sizes = (n_slab, n_grp, rows, slots, width, aggs)
    a_chunks = 7
    dma = pltpu.SemaphoreType.DMA
    scratch = [
        pltpu.SMEM((slots, rows), jnp.int32),
        pltpu.VMEM((1, rows), jnp.int32),
        pltpu.SMEM((1, half), jnp.int32),
        pltpu.VMEM((rows, slots, width, width), BF16),
        pltpu.VMEM((rows, width, slots * width), BF16),
        pltpu.VMEM((3 * rows, width, width), BF16),
        pltpu.VMEM((rows, width // 2, 2 * width), BF16),
        pltpu.VMEM((2, rows, width // 2, 2 * width), BF16),
        pltpu.VMEM((rows, width, width), BF16),
        pltpu.VMEM((aggs, width, width), BF16),
        pltpu.VMEM((aggs, width, width), BF16),
        pltpu.VMEM((rows + 1, width, width), F32),
        pltpu.VMEM((REACH, aggs, width // 2, 2 * width), BF16),
        pltpu.VMEM((2 * REACH + 1, aggs, width // 2, 2 * width), BF16),
        pltpu.VMEM((aggs, width // 2, 2 * width), F32),
        pltpu.VMEM((aggs, width // 2, 2 * width), F32),
        pltpu.VMEM((aggs, width, width), F32),
        pltpu.VMEM((half, width // 2, 2 * width), BF16),
        pltpu.VMEM((half, width // 2, 2 * width), BF16),
        pltpu.VMEM((8, 128), jnp.int32),
        pltpu.SMEM((8, 128), jnp.int32),
        dma((a_chunks,)),
        dma((CHUNKS,)),
        dma((5,)),
        dma,
        dma((2, CHUNKS)),
        dma((2, CHUNKS)),
        dma((REACH, 2)),
        dma((2 * REACH + 1, 2)),
        dma,
        dma((2,)),
        dma((2,)),
    ]
    vmem = pl.BlockSpec(memory_space=pltpu.VMEM)
    hbm = pl.BlockSpec(memory_space=pltpu.HBM)
    folded = pl.pallas_call(
        functools.partial(kernel, sizes),
        out_shape=(
            jax.ShapeDtypeStruct((aggs, width // 2, 2 * width), F32),
            jax.ShapeDtypeStruct((half, width // 2, 2 * width), F32),
        ),
        in_specs=[hbm] * 6,
        out_specs=(vmem, vmem),
        scratch_shapes=scratch,
        compiler_params=pltpu.CompilerParams(
            collective_id=0, has_side_effects=True, vmem_limit_bytes=30 * 2**20
        ),
    )(*(pltpu.with_memory_space_constraint(x, pltpu.HBM) for x in (neighbors.T, agg_ids.reshape(1, rows), pairing, a_blocks, prolong, coarse_prolong)))
    return pl.pallas_call(
        spread,
        out_shape=(
            jax.ShapeDtypeStruct((aggs, width, width), F32),
            jax.ShapeDtypeStruct((half, width, width), F32),
        ),
        in_specs=[vmem, vmem],
        out_specs=(hbm, hbm),
        scratch_shapes=[
            pltpu.VMEM((aggs, width, width), F32),
            pltpu.VMEM((half, width, width), F32),
            dma((2,)),
        ],
        compiler_params=pltpu.CompilerParams(vmem_limit_bytes=4 * 2**20),
    )(*folded)


def solution(mesh):
    placed = (
        P(("slab", "grp"), None, None, None),
        P(("slab", "grp"), None),
        P(("slab", "grp"), None, None),
        P(("slab", "grp")),
        P(("slab", "grp"), None, None),
        P(("slab", "grp"), None),
    )
    return jax.shard_map(
        functools.partial(on_device, mesh.shape["slab"], mesh.shape["grp"]),
        mesh=mesh,
        in_specs=placed,
        out_specs=(P(("slab", "grp"), None, None), P(("slab", "grp"), None, None)),
        check_vma=False,
    )
```
